32 devices in a mesh: dom: 16 (over z, y, x), rep: 2 (over core).
Axes of the slice: x: 2, y: 2, z: 4, core: 2. Of those that a mesh axis runs over, the one named last changes fastest.
Arguments:
- features: bfloat16 [4096, 256], P(('dom', 'rep')), may hold values from -6 to 6
- block_values: bfloat16 [32, 16, 2, 128, 128], P(('dom', 'rep'))
- block_columns: int32 [32, 16, 2], P(('dom', 'rep')), may hold values from 0 to 15, as said below
- weight: bfloat16 [256, 256], replicated, may hold values from -0.375 to 0.375
- cotangent: bfloat16 [4096, 256], P(('dom', 'rep')), may hold values from -6 to 6
Outputs:
- feature_grad: bfloat16 [4096, 256], P(('dom', 'rep'))
- weight_grad: float32 [256, 256], replicated
The draws below stay inside these ranges and needn't reach their ends.
Inputs may be any that keep to these rules, and one draw needn't show every extreme that they name: Slot (t, a) of the device with dom index d and rep index r lies at block row d * 2 + a and block column block_columns * 2 + r. The adjacency is symmetric: each slot at block row p and block column q has a partner slot of the same t at block row q and block column p whose block_values are its transpose; a slot with p equal to q holds a symmetric block.
All inputs are finite; a program needn't handle non-finite values.
Results may differ from the reference program's by a relative error of at most 0.006.
Values may be sent and summed in bfloat16 or wider, within the bound.
A program may use at most 64 MiB of HBM per device.

```python
import math
import jax
import jax.numpy as jnp
from jax import lax

F = 256
BLK = 128
ROUNDS = 16
NODES = 4096
N_DOM = 16
N_REP = 2


def sigma_table(key):
    round_keys = jax.random.split(jax.random.fold_in(key, 5), ROUNDS * N_REP * N_REP)

    def shuffle_one(one_key):
        return jax.random.permutation(one_key, N_DOM)
    shuffles = jax.vmap(shuffle_one)(round_keys).astype(jnp.int32).reshape(ROUNDS, N_REP, N_REP, N_DOM)
    inverse = jnp.argsort(shuffles, axis=-1, stable=True).astype(jnp.int32)
    shifts = jax.random.randint(jax.random.fold_in(key, 6), (ROUNDS, N_REP), 0, N_DOM, dtype=jnp.int32)
    dom_ids = jnp.arange(N_DOM, dtype=jnp.int32)
    mirror = (shifts[:, :, None] - dom_ids[None, None, :]) % N_DOM
    row_ids = jnp.arange(N_REP, dtype=jnp.int32)
    above_diag = (row_ids[:, None] < row_ids[None, :])[None, :, :, None]
    below_diag = (row_ids[:, None] > row_ids[None, :])[None, :, :, None]
    swapped = jnp.swapaxes(inverse, 1, 2)
    return jnp.where(above_diag, shuffles, jnp.where(below_diag, swapped, mirror[:, :, None, :]))


def column_table(key):
    return jnp.transpose(sigma_table(key), (3, 2, 0, 1))


def draw_block_columns(key, part):
    return column_table(key).reshape(N_DOM * N_REP, ROUNDS, N_REP).astype(jnp.int32)


def draw_block_values(key, part):
    columns = column_table(key)
    table_shape = columns.shape
    dom_ids = jnp.arange(N_DOM, dtype=jnp.int32)[:, None, None, None]
    rep_ids = jnp.arange(N_REP, dtype=jnp.int32)[None, :, None, None]
    round_ids = jnp.arange(ROUNDS, dtype=jnp.int32)[None, None, :, None]
    row_ids = jnp.arange(N_REP, dtype=jnp.int32)[None, None, None, :]
    row_block = dom_ids * N_REP + row_ids
    col_block = columns * N_REP + rep_ids
    low_block = jnp.minimum(row_block, col_block)
    high_block = jnp.maximum(row_block, col_block)
    pair_code = low_block * (N_DOM * N_REP) + high_block
    round_flat = jnp.broadcast_to(round_ids, table_shape).reshape(-1)
    code_flat = jnp.broadcast_to(pair_code, table_shape).reshape(-1)
    flip_flat = jnp.broadcast_to(row_block > col_block, table_shape).reshape(-1)
    diag_flat = jnp.broadcast_to(row_block == col_block, table_shape).reshape(-1)
    base_key = jax.random.fold_in(key, 9)

    def one_block(round_id, code, flipped, diagonal):
        block_key = jax.random.fold_in(jax.random.fold_in(base_key, round_id), code)
        drawn = jax.random.normal(block_key, (BLK, BLK), jnp.float32)
        turned = drawn.T
        return jnp.where(diagonal, (drawn + turned) * 0.7071067811865476, jnp.where(flipped, turned, drawn))
    blocks = jax.vmap(one_block)(round_flat, code_flat, flip_flat, diag_flat)
    value_scale = (ROUNDS * N_REP * BLK) ** (-0.5)
    return (blocks * value_scale).reshape(N_DOM * N_REP, ROUNDS, N_REP, BLK, BLK).astype(jnp.bfloat16)


def level_of(stream_key, dims, shards, low, top_value):
    loudness = 1.0
    for axis_at, shards_of in shards:
        heights = jax.random.uniform(jax.random.fold_in(jax.random.fold_in(stream_key, 6), axis_at), (shards_of,), jnp.float32, low / len(shards), top_value / len(shards))
        loudness = loudness * jnp.repeat(jnp.exp(heights), dims[axis_at] // shards_of).reshape((-1,) + (1,) * (len(dims) - 1 - axis_at))
    return loudness


def bell_draw(key, shape, deviation, limit, pieces=(), held_as=jnp.bfloat16):
    drawn = deviation * jax.random.normal(key, shape, jnp.float32)
    if pieces:
        drawn = drawn * level_of(key, shape, pieces, -0.22, 0.18)
    return jnp.clip(drawn, -limit, limit).astype(held_as)


def setup_inputs(seed: int = 0) -> dict:
    key_list = jax.random.split(jax.random.key(seed), 6)
    features = bell_draw(key_list[0], (NODES, F), 1.0, 6.0, ((0, 32),))
    block_values = draw_block_values(jax.random.fold_in(key_list[5], 71), 0)
    block_columns = draw_block_columns(jax.random.fold_in(key_list[5], 71), 0)
    weight = bell_draw(key_list[3], (F, F), F ** -0.5, 0.375)
    cotangent = bell_draw(key_list[4], (NODES, F), 1.0, 6.0, ((0, 32),))
    return {"features": features, "block_values": block_values, "block_columns": block_columns, "weight": weight, "cotangent": cotangent}


def apply_adjacency(node_field, values, columns):
    rep_ids = jnp.arange(N_REP, dtype=jnp.int32)

    def one_panel(operands):
        panel_values, panel_columns = operands
        picked = node_field[panel_columns, rep_ids[:, None, None]]
        return jnp.einsum('rtaij,rtajf->aif', panel_values.astype(jnp.float32), picked.astype(jnp.float32))
    result = lax.map(one_panel, (values, columns))
    return result.reshape(NODES, F)

def reference(features, block_values, block_columns, weight, cotangent):
    values = block_values.reshape(N_DOM, N_REP, ROUNDS, N_REP, BLK, BLK)
    columns = block_columns.reshape(N_DOM, N_REP, ROUNDS, N_REP)
    hidden = apply_adjacency(features.reshape(N_DOM, N_REP, BLK, F), values, columns).astype(jnp.bfloat16)
    pre_act = jnp.dot(hidden, weight, preferred_element_type=jnp.float32)
    sigmoid_value = jax.nn.sigmoid(pre_act)
    slope_value = sigmoid_value * (1.0 + pre_act * (1.0 - sigmoid_value))
    grad_pre = (cotangent.astype(jnp.float32) * slope_value).astype(jnp.bfloat16)
    weight_grad = jnp.dot(hidden.T, grad_pre, preferred_element_type=jnp.float32) * (1.0 / math.sqrt(NODES))
    hidden_grad = jnp.dot(grad_pre, weight.T, preferred_element_type=jnp.float32).astype(jnp.bfloat16)
    feature_grad = apply_adjacency(hidden_grad.reshape(N_DOM, N_REP, BLK, F), values, columns).astype(jnp.bfloat16)
    return (feature_grad, weight_grad)
```

```python
import functools
import math

import jax
import jax.numpy as jnp
from jax import lax
from jax.experimental import pallas as pl
from jax.experimental.pallas import tpu as pltpu
from jax.sharding import PartitionSpec as P

MESH = pl.DeviceIdType.MESH
FACE = 4
SUBLANES = 8


def flip(index, offset):
    result, bit = index, 1
    while bit <= offset:
        if offset & bit:
            result = result + bit - 2 * bit * ((index // bit) % 2)
        bit *= 2
    return result


def silu_slope(pre_act):
    sigmoid_value = jax.nn.sigmoid(pre_act)
    return sigmoid_value * (1.0 + pre_act * (1.0 - sigmoid_value))


class Sends:
    def __init__(self):
        self.started = []

    def start(self, src, dst, send_sem, recv_sem, target):
        copy = pltpu.make_async_remote_copy(
            src_ref=src, dst_ref=dst, send_sem=send_sem, recv_sem=recv_sem,
            device_id=target, device_id_type=MESH,
        )
        copy.start()
        self.started.append(copy)

    def finish(self):
        for copy in self.started:
            copy.wait_send()


def arrived(ref, send_sem, recv_sem, target):
    pltpu.make_async_remote_copy(
        src_ref=ref, dst_ref=ref, send_sem=send_sem, recv_sem=recv_sem,
        device_id=target, device_id_type=MESH,
    ).wait_recv()


def kernel(
    n_dom, n_rep, inv_scale,
    columns_ref, features_ref, values_hbm, weight_ref, cotangent_ref,
    feature_grad_ref, weight_grad_ref,
    values_ref, panels, grad_panels, own_grad, part_out, part_in,
    weight_part, weight_in1, weight_sum1, weight_in2, weight_sum2, weight_in3, weight_out,
    values_sem, gather_send, gather_recv, part_send, part_recv, weight_send, weight_recv,
):
    rows = features_ref.shape[0]
    half = rows // 2
    rounds = values_ref.shape[0]
    line = n_dom // FACE
    dom, rep = lax.axis_index("dom"), lax.axis_index("rep")
    z, face = dom // FACE, dom % FACE

    def panel_at(z_at, face_at):
        return z_at * FACE + face_at

    line_ids = [panel_at(flip(z, k), face) for k in range(line)]
    face_ids = [panel_at(z, flip(face, j)) for j in range(FACE)]
    rep_ids = [lax.rem(rep + k, n_rep) for k in range(n_rep)]
    from_rep_ids = [lax.rem(rep - k + n_rep, n_rep) for k in range(n_rep)]
    line_to = [{"dom": i} for i in line_ids]
    face_to = [{"dom": i} for i in face_ids]
    rep_to = [{"rep": i} for i in rep_ids]

    values_copy = pltpu.make_async_copy(values_hbm.at[0], values_ref, values_sem)
    values_copy.start()

    barrier = pltpu.get_barrier_semaphore()
    partners = line_to[1:] + face_to[1:] + rep_to[1:]
    for target in partners:
        pl.semaphore_signal(barrier, inc=1, device_id=target, device_id_type=MESH)
    pl.semaphore_wait(barrier, len(partners))

    sends = Sends()

    def gather(which, own_ref, held):
        send_sem, recv_sem = gather_send.at[which], gather_recv.at[which]
        line_at, full_at, half_at = 0, (line, 2 * line), (3 * line, 4 * line)
        halves = (pl.ds(0, half), pl.ds(half, half))

        def sem_pair(at):
            return send_sem.at[at], recv_sem.at[at]

        def to_neighbours(k):
            panel = line_ids[k]
            src = own_ref if k == 0 else held.at[panel]
            for way in range(2):
                sends.start(src, held.at[panel], *sem_pair(full_at[way] + k), face_to[way + 1])

        def to_diagonal(k):
            for way in range(2):
                panel = panel_at(flip(z, k), flip(face, way + 1))
                arrived(held.at[panel], *sem_pair(full_at[way] + k), face_to[way + 1])
                piece = held.at[panel, halves[way]]
                sends.start(piece, piece, *sem_pair(half_at[1 - way] + k), face_to[2 - way])

        def begin():
            for k in range(1, line):
                sends.start(own_ref, held.at[dom], *sem_pair(line_at + k), line_to[k])
            to_neighbours(0)
            held[dom] = own_ref[...]

        def middle(k):
            arrived(held.at[line_ids[k]], *sem_pair(line_at + k), line_to[k])
            to_neighbours(k)
            to_diagonal(k - 1)

        def finish():
            for k in range(line):
                panel = panel_at(flip(z, k), flip(face, 3))
                for way in range(2):
                    arrived(held.at[panel, halves[1 - way]], *sem_pair(half_at[way] + k), face_to[way + 1])

        steps = [begin]
        steps += [functools.partial(middle, k) for k in range(1, line)]
        steps += [functools.partial(to_diagonal, line - 1), finish]
        return steps

    def block_product(held, a):
        left = jnp.concatenate([values_ref[t, a] for t in range(rounds)], axis=1)
        right = jnp.concatenate([held[columns_ref[0, t, a]] for t in range(rounds)], axis=0)
        return jnp.dot(left, right, preferred_element_type=jnp.float32)

    def panel_start(which, held):
        for k in range(1, n_rep):
            part_out[which, k - 1] = block_product(held, rep_ids[k])
            sends.start(
                part_out.at[which, k - 1], part_in.at[which, k - 1],
                part_send.at[which, k - 1], part_recv.at[which, k - 1], rep_to[k],
            )
        return block_product(held, rep)

    def panel_end(which, total):
        for k in range(1, n_rep):
            arrived(
                part_in.at[which, k - 1], part_send.at[which, k - 1],
                part_recv.at[which, k - 1], rep_to[k],
            )
            total = total + part_in[which, k - 1]
        return total.astype(jnp.bfloat16)

    for step in gather(0, features_ref, panels):
        step()
    values_copy.wait()
    hidden = panel_end(0, panel_start(0, panels))

    weight = weight_ref[...]
    pre_act = jnp.dot(hidden, weight, preferred_element_type=jnp.float32)
    grad_pre = (cotangent_ref[...].astype(jnp.float32) * silu_slope(pre_act)).astype(jnp.bfloat16)
    own_grad[...] = lax.dot_general(
        grad_pre, weight, (((1,), (1,)), ((), ())), preferred_element_type=jnp.float32
    ).astype(jnp.bfloat16)
    back = gather(1, own_grad, grad_panels)
    back[0]()

    rep_rows = weight.shape[0] // n_rep
    line_rows = rep_rows // line
    face_rows = line_rows // FACE
    rep_base = rep * rep_rows
    line_base = rep_base + z * line_rows
    sem_at = [0]

    def weight_sems(count):
        base = sem_at[0]
        sem_at[0] += count - 1
        return [(weight_send.at[base + k - 1], weight_recv.at[base + k - 1]) for k in range(1, count)]

    def span(start, size):
        return pl.ds(pl.multiple_of(start, SUBLANES), size)

    def exchange(out_ref, in_ref, targets, ids, size):
        sems = weight_sems(len(targets))
        for k in range(1, len(targets)):
            sends.start(out_ref.at[span(ids[k] * size, size)], in_ref.at[k - 1], *sems[k - 1], targets[k])
        return sems

    def take(in_ref, sems, targets, total):
        for k in range(1, len(targets)):
            arrived(in_ref.at[k - 1], *sems[k - 1], targets[k])
            total = total + in_ref[k - 1]
        return total

    def share(start, size, targets):
        sems = weight_sems(len(targets))
        piece = weight_out.at[span(start, size)]
        for k in range(1, len(targets)):
            sends.start(piece, piece, *sems[k - 1], targets[k])
        return sems

    def collect(starts, size, sems, targets):
        for k in range(1, len(targets)):
            arrived(weight_out.at[span(starts[k], size)], *sems[k - 1], targets[k])

    line_z = [flip(z, k) for k in range(line)]
    face_f = [flip(face, j) for j in range(FACE)]

    weight_part[...] = lax.dot_general(
        hidden, grad_pre, (((0,), (0,)), ((), ())), preferred_element_type=jnp.float32
    )
    sems1 = exchange(weight_part, weight_in1, rep_to, rep_ids, rep_rows)
    back[1]()
    weight_sum1[...] = take(weight_in1, sems1, rep_to, weight_part[span(rep_base, rep_rows)])
    sems2 = exchange(weight_sum1, weight_in2, line_to, line_z, line_rows)
    for step in back[2:line]:
        step()
    weight_sum2[...] = take(weight_in2, sems2, line_to, weight_sum1[span(z * line_rows, line_rows)])
    sems3 = exchange(weight_sum2, weight_in3, face_to, face_f, face_rows)
    back[line]()
    own_sum = take(weight_in3, sems3, face_to, weight_sum2[span(face * face_rows, face_rows)])
    own_base = line_base + face * face_rows
    weight_out[span(own_base, face_rows)] = own_sum * inv_scale
    sems4 = share(own_base, face_rows, face_to)
    back[line + 1]()
    collect([line_base + f * face_rows for f in face_f], face_rows, sems4, face_to)
    sems5 = share(line_base, line_rows, line_to)

    total = panel_start(1, grad_panels)
    collect([rep_base + i * line_rows for i in line_z], line_rows, sems5, line_to)
    sems6 = share(rep_base, rep_rows, rep_to)
    feature_grad_ref[...] = panel_end(1, total)
    collect([i * rep_rows for i in from_rep_ids], rep_rows, sems6, rep_to)
    weight_grad_ref[...] = weight_out[...]
    sends.finish()


def kernel_shards(features, block_values, block_columns, weight, cotangent):
    n_dom, n_rep = lax.axis_size("dom"), lax.axis_size("rep")
    rows, width = features.shape
    _, rounds, _, blk, _ = block_values.shape
    wide = weight.shape[0]
    line = n_dom // FACE
    rep_rows = wide // n_rep
    line_rows = rep_rows // line
    face_rows = line_rows // FACE
    inv_scale = 1.0 / math.sqrt(rows * n_dom * n_rep)
    gather_copies = 5 * line
    weight_copies = 2 * ((n_rep - 1) + (line - 1) + (FACE - 1))
    vmem = pl.BlockSpec(memory_space=pltpu.VMEM)
    dma = pltpu.SemaphoreType.DMA
    parts = max(n_rep - 1, 1)
    return pl.pallas_call(
        functools.partial(kernel, n_dom, n_rep, inv_scale),
        out_shape=(
            jax.ShapeDtypeStruct((rows, width), jnp.bfloat16),
            jax.ShapeDtypeStruct(weight.shape, jnp.float32),
        ),
        in_specs=[
            pl.BlockSpec(memory_space=pltpu.SMEM), vmem, pl.BlockSpec(memory_space=pl.ANY), vmem, vmem,
        ],
        out_specs=(vmem, vmem),
        scratch_shapes=[
            pltpu.VMEM(block_values.shape[1:], jnp.bfloat16),
            pltpu.VMEM((n_dom, rows, width), jnp.bfloat16),
            pltpu.VMEM((n_dom, rows, width), jnp.bfloat16),
            pltpu.VMEM((rows, width), jnp.bfloat16),
            pltpu.VMEM((2, parts, rows, width), jnp.float32),
            pltpu.VMEM((2, parts, rows, width), jnp.float32),
            pltpu.VMEM(weight.shape, jnp.float32),
            pltpu.VMEM((parts, rep_rows, wide), jnp.float32),
            pltpu.VMEM((rep_rows, wide), jnp.float32),
            pltpu.VMEM((max(line - 1, 1), line_rows, wide), jnp.float32),
            pltpu.VMEM((line_rows, wide), jnp.float32),
            pltpu.VMEM((FACE - 1, face_rows, wide), jnp.float32),
            pltpu.VMEM(weight.shape, jnp.float32),
            dma,
            dma((2, gather_copies)),
            dma((2, gather_copies)),
            dma((2, parts)),
            dma((2, parts)),
            dma((weight_copies,)),
            dma((weight_copies,)),
        ],
        compiler_params=pltpu.CompilerParams(
            collective_id=0, has_side_effects=True, vmem_limit_bytes=32 * 1024 * 1024
        ),
    )(block_columns, features, block_values, weight, cotangent)


def panel_product(values, columns, gathered, block_rows):
    panel_count = gathered.shape[0] // block_rows
    panels = gathered.reshape(panel_count, block_rows, gathered.shape[1])
    picked = panels[columns]
    summed = jnp.einsum("taij,tajf->aif", values, picked, preferred_element_type=jnp.float32)
    return summed.reshape(-1, summed.shape[-1])


def plain_shards(features, block_values, block_columns, weight, cotangent):
    block_rows = features.shape[0]
    values, columns = block_values[0], block_columns[0]
    gathered = lax.all_gather(features, "dom", axis=0, tiled=True)
    inv_scale = 1.0 / math.sqrt(gathered.shape[0] * lax.axis_size("rep"))
    partial_value = panel_product(values, columns, gathered, block_rows)
    hidden = lax.psum_scatter(partial_value, "rep", scatter_dimension=0, tiled=True).astype(jnp.bfloat16)
    pre_act = jnp.dot(hidden, weight, preferred_element_type=jnp.float32)
    grad_pre = (cotangent.astype(jnp.float32) * silu_slope(pre_act)).astype(jnp.bfloat16)
    hidden_grad = jnp.einsum(
        "rg,fg->rf", grad_pre, weight, preferred_element_type=jnp.float32
    ).astype(jnp.bfloat16)
    weight_part = jnp.einsum("rf,rg->fg", hidden, grad_pre, preferred_element_type=jnp.float32)
    weight_grad = lax.psum(weight_part, ("dom", "rep")) * inv_scale
    grad_rows = lax.all_gather(hidden_grad, "dom", axis=0, tiled=True)
    back_partial = panel_product(values, columns, grad_rows, block_rows)
    feature_grad = lax.psum_scatter(back_partial, "rep", scatter_dimension=0, tiled=True)
    return (feature_grad.astype(jnp.bfloat16), weight_grad)


def shards(features, block_values, block_columns, weight, cotangent):
    n_dom, n_rep = lax.axis_size("dom"), lax.axis_size("rep")
    line = n_dom // FACE
    splits = (
        n_dom % FACE == 0
        and line & (line - 1) == 0
        and weight.shape[0] % (SUBLANES * n_dom * n_rep) == 0
    )
    body = kernel_shards if splits else plain_shards
    return body(features, block_values, block_columns, weight, cotangent)


def solution(mesh):
    return jax.shard_map(
        shards,
        mesh=mesh,
        in_specs=(
            P(("dom", "rep"), None),
            P(("dom", "rep"), None, None, None, None),
            P(("dom", "rep"), None, None),
            P(),
            P(("dom", "rep"), None),
        ),
        out_specs=(P(("dom", "rep"), None), P()),
        check_vma=False,
    )
```

```python
import functools
import math

import jax
import jax.numpy as jnp
from jax import lax
from jax.experimental import pallas as pl
from jax.experimental.pallas import tpu as pltpu
from jax.sharding import PartitionSpec as P

MESH = pl.DeviceIdType.MESH
FACE = 4
SUBLANES = 16
LANES = 128
CHUNKS = 2
VMEM_BYTES = 60 * 1024 * 1024


def flip(index, offset):
    result, bit = index, 1
    while bit <= offset:
        if offset & bit:
            result = result + bit - 2 * bit * ((index // bit) % 2)
        bit *= 2
    return result


def silu_slope(pre_act):
    sigmoid_value = jax.nn.sigmoid(pre_act)
    return sigmoid_value * (1.0 + pre_act * (1.0 - sigmoid_value))


class Sends:
    def __init__(self):
        self.started = []

    def start(self, src, dst, send_sem, recv_sem, target, cond=None):
        def make():
            return pltpu.make_async_remote_copy(
                src_ref=src, dst_ref=dst, send_sem=send_sem, recv_sem=recv_sem,
                device_id=target, device_id_type=MESH,
            )

        when(cond, lambda: make().start())
        self.started.append((cond, make))

    def finish(self):
        for cond, make in self.started:
            when(cond, lambda make=make: make().wait_send())


def when(cond, action):
    if cond is None:
        action()
    else:
        pl.when(cond)(action)


def arrived(ref, send_sem, recv_sem, target):
    pltpu.make_async_remote_copy(
        src_ref=ref, dst_ref=ref, send_sem=send_sem, recv_sem=recv_sem,
        device_id=target, device_id_type=MESH,
    ).wait_recv()


def kernel(
    n_dom, n_rep, inv_scale,
    columns_ref, features_hbm, values_hbm, weight_hbm, cotangent_hbm,
    feature_grad_ref, weight_grad_ref,
    values_ref, weight_ref, cotangent_ref, panels, grad_panels, part_out, part_in,
    weight_part, weight_in1, weight_sum1, weight_in2, weight_sum2, weight_in3, weight_out,
    local_sem, line_send, line_recv, full_send, full_recv, half_send, half_recv,
    part_send, part_recv, weight_send, weight_recv,
):
    rows = cotangent_ref.shape[0]
    rounds = values_ref.shape[0]
    line = n_dom // FACE
    dom, rep = lax.axis_index("dom"), lax.axis_index("rep")
    z, face = dom // FACE, dom % FACE

    def panel_at(z_at, face_at):
        return z_at * FACE + face_at

    line_ids = [panel_at(flip(z, k), face) for k in range(line)]
    face_ids = [panel_at(z, flip(face, j)) for j in range(FACE)]
    rep_ids = [lax.rem(rep + k, n_rep) for k in range(n_rep)]
    from_rep_ids = [lax.rem(rep - k + n_rep, n_rep) for k in range(n_rep)]
    line_to = [{"dom": i} for i in line_ids]
    face_to = [{"dom": i} for i in face_ids]
    rep_to = [{"rep": i} for i in rep_ids]

    local = [
        pltpu.make_async_copy(src, dst, local_sem.at[i])
        for i, (src, dst) in enumerate((
            (features_hbm, panels.at[dom]),
            (values_hbm.at[0], values_ref),
            (weight_hbm, weight_ref),
            (cotangent_hbm, cotangent_ref),
        ))
    ]
    for copy in local:
        copy.start()

    barrier = pltpu.get_barrier_semaphore()
    partners = line_to[1:] + face_to[1:] + rep_to[1:]
    for target in partners:
        pl.semaphore_signal(barrier, inc=1, device_id=target, device_id_type=MESH)
    local[0].wait()
    pl.semaphore_wait(barrier, len(partners))

    sends = Sends()
    chunk = rows // CHUNKS
    half = chunk // 2

    def gather(which, held):
        def source(way, s):
            at = 0 if s == 0 else 1 + 2 * (s - 1) + way
            z_at = z - s if way == 0 else z + s
            if s == 0:
                here = None
            else:
                here = z >= s if way == 0 else z + s < line
            return at, z_at, here

        def sources(s):
            return [source(way, s) for way in range(1 if s == 0 else 2)]

        def rows_of(c):
            return pl.ds(c * chunk, chunk)

        def half_of(c, way):
            return pl.ds(c * chunk + way * half, half)

        def both(first, second):
            return second if first is None else jnp.logical_and(first, second)

        def along(way, s, c):
            at, z_at, here = source(way, s)
            onward = z + 1 < line if way == 0 else z >= 1
            piece = held.at[panel_at(z_at, face), rows_of(c)]
            slot = (which, way, s, c)
            target = {"dom": dom + FACE if way == 0 else dom - FACE}
            sends.start(piece, piece, line_send.at[slot], line_recv.at[slot], target, both(here, onward))

        def to_neighbours(found, c):
            at, z_at, here = found
            piece = held.at[panel_at(z_at, face), rows_of(c)]
            for way in range(2):
                slot = (which, way, at, c)
                sends.start(piece, piece, full_send.at[slot], full_recv.at[slot], face_to[way + 1], here)

        def to_diagonal(s, c):
            for at, z_at, here in sources(s):
                for way in range(2):
                    panel = panel_at(z_at, flip(face, way + 1))
                    slot = (which, way, at, c)
                    piece = held.at[panel, rows_of(c)]
                    when(here, lambda piece=piece, slot=slot, way=way: arrived(
                        piece, full_send.at[slot], full_recv.at[slot], face_to[way + 1]))
                    piece = held.at[panel, half_of(c, way)]
                    slot = (which, 1 - way, at, c)
                    sends.start(piece, piece, half_send.at[slot], half_recv.at[slot], face_to[2 - way], here)

        def begin():
            for c in range(CHUNKS):
                for way in range(2):
                    along(way, 0, c)
                to_neighbours(source(0, 0), c)

        def middle(s):
            for c in range(CHUNKS):
                for way in range(2):
                    found = source(way, s)
                    piece = held.at[panel_at(found[1], face), rows_of(c)]
                    slot = (which, way, s - 1, c)
                    when(found[2], lambda piece=piece, slot=slot: arrived(
                        piece, line_send.at[slot], line_recv.at[slot], {"dom": dom}))
                    if s + 1 < line:
                        along(way, s, c)
                    to_neighbours(found, c)
                to_diagonal(s - 1, c)

        def last():
            for c in range(CHUNKS):
                to_diagonal(line - 1, c)

        def finish():
            for s in range(line):
                for at, z_at, here in sources(s):
                    for c in range(CHUNKS):
                        for way in range(2):
                            piece = held.at[panel_at(z_at, flip(face, 3)), half_of(c, 1 - way)]
                            slot = (which, way, at, c)
                            when(here, lambda piece=piece, slot=slot, way=way: arrived(
                                piece, half_send.at[slot], half_recv.at[slot], face_to[way + 1]))

        steps = [begin]
        steps += [functools.partial(middle, s) for s in range(1, line)]
        steps += [last, finish]
        return steps

    def block_product(held, a):
        left = jnp.concatenate([values_ref[t, a] for t in range(rounds)], axis=1)
        right = jnp.concatenate([held[columns_ref[0, a, t]] for t in range(rounds)], axis=0)
        return jnp.dot(left, right, preferred_element_type=jnp.float32)

    def panel_start(which, held):
        for k in range(1, n_rep):
            part_out[which, k - 1] = block_product(held, rep_ids[k])
            sends.start(
                part_out.at[which, k - 1], part_in.at[which, k - 1],
                part_send.at[which, k - 1], part_recv.at[which, k - 1], rep_to[k],
            )
        return block_product(held, rep)

    def panel_end(which, total):
        for k in range(1, n_rep):
            arrived(
                part_in.at[which, k - 1], part_send.at[which, k - 1],
                part_recv.at[which, k - 1], rep_to[k],
            )
            total = total + part_in[which, k - 1]
        return total.astype(jnp.bfloat16)

    for step in gather(0, panels):
        step()
    for copy in local[1:]:
        copy.wait()
    hidden = panel_end(0, panel_start(0, panels))

    weight = weight_ref[...]
    pre_act = jnp.dot(hidden, weight, preferred_element_type=jnp.float32)
    grad_pre = (cotangent_ref[...].astype(jnp.float32) * silu_slope(pre_act)).astype(jnp.bfloat16)
    grad_panels[dom] = lax.dot_general(
        grad_pre, weight, (((1,), (1,)), ((), ())), preferred_element_type=jnp.float32
    ).astype(jnp.bfloat16)
    back = gather(1, grad_panels)
    back[0]()

    wide = weight.shape[0]
    rep_rows = wide // n_rep
    line_rows = rep_rows // line
    face_rows, face_columns = line_rows // 2, wide // 2
    rep_base = rep * rep_rows
    line_base = rep_base + z * line_rows
    sem_at = [0]

    def weight_sems(count):
        base = sem_at[0]
        sem_at[0] += count - 1
        return [(weight_send.at[base + k - 1], weight_recv.at[base + k - 1]) for k in range(1, count)]

    def span(start, size):
        return (pl.ds(pl.multiple_of(start, SUBLANES), size),)

    def tile(start, f):
        return (
            pl.ds(pl.multiple_of(start + (f // 2) * face_rows, SUBLANES), face_rows),
            pl.ds(pl.multiple_of((f % 2) * face_columns, LANES), face_columns),
        )

    def exchange(out_ref, in_ref, targets, pieces):
        sems = weight_sems(len(targets))
        for k in range(1, len(targets)):
            sends.start(out_ref.at[pieces[k]], in_ref.at[k - 1], *sems[k - 1], targets[k])
        return sems

    def take(in_ref, sems, targets, total):
        for k in range(1, len(targets)):
            arrived(in_ref.at[k - 1], *sems[k - 1], targets[k])
            total = total + in_ref[k - 1]
        return total

    def share(piece, targets):
        sems = weight_sems(len(targets))
        for k in range(1, len(targets)):
            sends.start(weight_out.at[piece], weight_out.at[piece], *sems[k - 1], targets[k])
        return sems

    def collect(pieces, sems, targets):
        for k in range(1, len(targets)):
            arrived(weight_out.at[pieces[k]], *sems[k - 1], targets[k])

    line_z = [flip(z, k) for k in range(line)]
    face_f = [flip(face, j) for j in range(FACE)]

    weight_part[...] = lax.dot_general(
        hidden, grad_pre, (((0,), (0,)), ((), ())), preferred_element_type=jnp.float32
    )
    sems1 = exchange(weight_part, weight_in1, rep_to, [span(i * rep_rows, rep_rows) for i in rep_ids])
    back[1]()
    weight_sum1[...] = take(weight_in1, sems1, rep_to, weight_part[span(rep_base, rep_rows)])
    sems2 = exchange(weight_sum1, weight_in2, line_to, [span(i * line_rows, line_rows) for i in line_z])
    for step in back[2:line]:
        step()
    weight_sum2[...] = take(weight_in2, sems2, line_to, weight_sum1[span(z * line_rows, line_rows)])
    sems3 = exchange(weight_sum2, weight_in3, face_to, [tile(0, f) for f in face_f])
    back[line]()
    own_sum = take(weight_in3, sems3, face_to, weight_sum2[tile(0, face)])
    weight_out[tile(line_base, face)] = (own_sum * inv_scale).astype(jnp.bfloat16)
    sems4 = share(tile(line_base, face), face_to)
    back[line + 1]()
    collect([tile(line_base, f) for f in face_f], sems4, face_to)
    sems5 = share(span(line_base, line_rows), line_to)

    total = panel_start(1, grad_panels)
    collect([span(rep_base + i * line_rows, line_rows) for i in line_z], sems5, line_to)
    sems6 = share(span(rep_base, rep_rows), rep_to)
    feature_grad_ref[...] = panel_end(1, total)
    collect([span(i * rep_rows, rep_rows) for i in from_rep_ids], sems6, rep_to)
    weight_grad_ref[...] = weight_out[...]
    sends.finish()


def kernel_shards(features, block_values, block_columns, weight, cotangent):
    n_dom, n_rep = lax.axis_size("dom"), lax.axis_size("rep")
    rows, width = features.shape
    wide = weight.shape[0]
    line = n_dom // FACE
    rep_rows = wide // n_rep
    line_rows = rep_rows // line
    inv_scale = 1.0 / math.sqrt(rows * n_dom * n_rep)
    weight_copies = 2 * ((n_rep - 1) + (line - 1) + (FACE - 1))
    parts, steps = max(n_rep - 1, 1), max(line - 1, 1)
    vmem = pl.BlockSpec(memory_space=pltpu.VMEM)
    any_space = pl.BlockSpec(memory_space=pl.ANY)
    dma = pltpu.SemaphoreType.DMA
    face_slots = (2, 2, 2 * line - 1, CHUNKS)
    line_slots = (2, 2, steps, CHUNKS)
    feature_grad, weight_grad = pl.pallas_call(
        functools.partial(kernel, n_dom, n_rep, inv_scale),
        out_shape=(
            jax.ShapeDtypeStruct((rows, width), jnp.bfloat16),
            jax.ShapeDtypeStruct(weight.shape, jnp.bfloat16),
        ),
        in_specs=[pl.BlockSpec(memory_space=pltpu.SMEM)] + [any_space] * 4,
        out_specs=(vmem, vmem),
        scratch_shapes=[
            pltpu.VMEM(block_values.shape[1:], jnp.bfloat16),
            pltpu.VMEM(weight.shape, jnp.bfloat16),
            pltpu.VMEM(cotangent.shape, jnp.bfloat16),
            pltpu.VMEM((n_dom, rows, width), jnp.bfloat16),
            pltpu.VMEM((n_dom, rows, width), jnp.bfloat16),
            pltpu.VMEM((2, parts, rows, width), jnp.float32),
            pltpu.VMEM((2, parts, rows, width), jnp.float32),
            pltpu.VMEM(weight.shape, jnp.float32),
            pltpu.VMEM((parts, rep_rows, wide), jnp.float32),
            pltpu.VMEM((rep_rows, wide), jnp.float32),
            pltpu.VMEM((steps, line_rows, wide), jnp.float32),
            pltpu.VMEM((line_rows, wide), jnp.float32),
            pltpu.VMEM((FACE - 1, line_rows // 2, wide // 2), jnp.float32),
            pltpu.VMEM(weight.shape, jnp.bfloat16),
            dma((4,)),
            dma(line_slots), dma(line_slots),
            dma(face_slots), dma(face_slots),
            dma(face_slots), dma(face_slots),
            dma((2, parts)), dma((2, parts)),
            dma((weight_copies,)), dma((weight_copies,)),
        ],
        compiler_params=pltpu.CompilerParams(
            collective_id=0, has_side_effects=True, vmem_limit_bytes=VMEM_BYTES
        ),
    )(jnp.swapaxes(block_columns, 1, 2), features, block_values, weight, cotangent)
    return feature_grad, weight_grad.astype(jnp.float32)


def panel_product(values, columns, gathered, block_rows):
    panel_count = gathered.shape[0] // block_rows
    panels = gathered.reshape(panel_count, block_rows, gathered.shape[1])
    picked = panels[columns]
    summed = jnp.einsum("taij,tajf->aif", values, picked, preferred_element_type=jnp.float32)
    return summed.reshape(-1, summed.shape[-1])


def plain_shards(features, block_values, block_columns, weight, cotangent):
    block_rows = features.shape[0]
    values, columns = block_values[0], block_columns[0]
    gathered = lax.all_gather(features, "dom", axis=0, tiled=True)
    inv_scale = 1.0 / math.sqrt(gathered.shape[0] * lax.axis_size("rep"))
    partial_value = panel_product(values, columns, gathered, block_rows)
    hidden = lax.psum_scatter(partial_value, "rep", scatter_dimension=0, tiled=True).astype(jnp.bfloat16)
    pre_act = jnp.dot(hidden, weight, preferred_element_type=jnp.float32)
    grad_pre = (cotangent.astype(jnp.float32) * silu_slope(pre_act)).astype(jnp.bfloat16)
    hidden_grad = jnp.einsum(
        "rg,fg->rf", grad_pre, weight, preferred_element_type=jnp.float32
    ).astype(jnp.bfloat16)
    weight_part = jnp.einsum("rf,rg->fg", hidden, grad_pre, preferred_element_type=jnp.float32)
    weight_grad = lax.psum(weight_part, ("dom", "rep")) * inv_scale
    grad_rows = lax.all_gather(hidden_grad, "dom", axis=0, tiled=True)
    back_partial = panel_product(values, columns, grad_rows, block_rows)
    feature_grad = lax.psum_scatter(back_partial, "rep", scatter_dimension=0, tiled=True)
    return (feature_grad.astype(jnp.bfloat16), weight_grad)


def shards(features, block_values, block_columns, weight, cotangent):
    n_dom, n_rep = lax.axis_size("dom"), lax.axis_size("rep")
    line = n_dom // FACE
    splits = (
        n_dom % FACE == 0
        and line & (line - 1) == 0
        and weight.shape[0] % (2 * SUBLANES * line * n_rep) == 0
        and weight.shape[0] % (2 * LANES) == 0
        and features.shape[0] % (2 * SUBLANES * CHUNKS) == 0
    )
    body = kernel_shards if splits else plain_shards
    return body(features, block_values, block_columns, weight, cotangent)


def solution(mesh):
    return jax.shard_map(
        shards,
        mesh=mesh,
        in_specs=(
            P(("dom", "rep"), None),
            P(("dom", "rep"), None, None, None, None),
            P(("dom", "rep"), None, None),
            P(),
            P(("dom", "rep"), None),
        ),
        out_specs=(P(("dom", "rep"), None), P()),
        check_vma=False,
    )
```

```python
import functools
import math

import jax
import jax.numpy as jnp
from jax import lax
from jax.experimental import pallas as pl
from jax.experimental.pallas import tpu as pltpu
from jax.sharding import PartitionSpec as P

MESH = pl.DeviceIdType.MESH
FACE = 4
SUBLANES = 16
LANES = 128
VMEM_BYTES = 60 * 1024 * 1024


def flip(index, offset):
    result, bit = index, 1
    while bit <= offset:
        if offset & bit:
            result = result + bit - 2 * bit * ((index // bit) % 2)
        bit *= 2
    return result


def silu_slope(pre_act):
    sigmoid_value = jax.nn.sigmoid(pre_act)
    return sigmoid_value * (1.0 + pre_act * (1.0 - sigmoid_value))


class Sends:
    def __init__(self):
        self.started = []

    def start(self, src, dst, send_sem, recv_sem, target):
        copy = pltpu.make_async_remote_copy(
            src_ref=src, dst_ref=dst, send_sem=send_sem, recv_sem=recv_sem,
            device_id=target, device_id_type=MESH,
        )
        copy.start()
        self.started.append(copy)
        return copy

    def left(self, copy):
        copy.wait_send()
        self.started = [other for other in self.started if other is not copy]

    def finish(self):
        for copy in self.started:
            copy.wait_send()


def arrived(ref, send_sem, recv_sem, target):
    pltpu.make_async_remote_copy(
        src_ref=ref, dst_ref=ref, send_sem=send_sem, recv_sem=recv_sem,
        device_id=target, device_id_type=MESH,
    ).wait_recv()


def kernel(
    n_dom, n_rep, inv_scale,
    columns_ref, features_hbm, values_hbm, weight_hbm, cotangent_hbm,
    feature_grad_ref, weight_grad_ref,
    values_ref, weight_ref, cotangent_ref, panels, grad_panels, part_out, part_in,
    weight_part, weight_in1, weight_sum1, weight_in2, weight_sum2, weight_in3, weight_out,
    local_sem, line_send, line_recv, full_send, full_recv, half_send, half_recv,
    part_send, part_recv, weight_send, weight_recv,
):
    rows = cotangent_ref.shape[0]
    rounds = values_ref.shape[0]
    line = n_dom // FACE
    dom, rep = lax.axis_index("dom"), lax.axis_index("rep")
    z, face = dom // FACE, dom % FACE

    def panel_at(z_at, face_at):
        return z_at * FACE + face_at

    line_ids = [panel_at(flip(z, k), face) for k in range(line)]
    face_ids = [panel_at(z, flip(face, j)) for j in range(FACE)]
    rep_ids = [lax.rem(rep + k, n_rep) for k in range(n_rep)]
    from_rep_ids = [lax.rem(rep - k + n_rep, n_rep) for k in range(n_rep)]
    line_to = [{"dom": i} for i in line_ids]
    face_to = [{"dom": i} for i in face_ids]
    rep_to = [{"rep": i} for i in rep_ids]

    local = [
        pltpu.make_async_copy(src, dst, local_sem.at[i])
        for i, (src, dst) in enumerate((
            (features_hbm, panels.at[dom]),
            (values_hbm.at[0], values_ref),
            (weight_hbm, weight_ref),
            (cotangent_hbm, cotangent_ref),
        ))
    ]
    for copy in local:
        copy.start()

    barrier = pltpu.get_barrier_semaphore()
    partners = line_to[1:] + face_to[1:] + rep_to[1:]
    for target in partners:
        pl.semaphore_signal(barrier, inc=1, device_id=target, device_id_type=MESH)
    local[0].wait()
    pl.semaphore_wait(barrier, len(partners))

    sends = Sends()
    half = rows // 2

    def gather(which, held):
        halves = (pl.ds(0, half), pl.ds(half, half))

        def along(k):
            own = held.at[dom]
            return sends.start(own, own, line_send.at[which, k - 1], line_recv.at[which, k - 1], line_to[k])

        def next_along(k):
            if k < line:
                sends.left(pending.pop())
                pending.append(along(k))

        pending = []

        def to_neighbours(k):
            piece = held.at[line_ids[k]]
            for way in range(2):
                slot = (which, way, k)
                sends.start(piece, piece, full_send.at[slot], full_recv.at[slot], face_to[way + 1])

        def to_diagonal(k):
            for way in range(2):
                panel = panel_at(flip(z, k), flip(face, way + 1))
                slot = (which, way, k)
                arrived(held.at[panel], full_send.at[slot], full_recv.at[slot], face_to[way + 1])
                piece = held.at[panel, halves[way]]
                slot = (which, 1 - way, k)
                sends.start(piece, piece, half_send.at[slot], half_recv.at[slot], face_to[2 - way])

        def begin():
            if line > 1:
                pending.append(along(1))
            to_neighbours(0)

        def own_diagonal():
            next_along(2)
            to_diagonal(0)

        def middle(k):
            arrived(held.at[line_ids[k]], line_send.at[which, k - 1], line_recv.at[which, k - 1], line_to[k])
            to_neighbours(k)
            next_along(k + 2)
            if k > 1:
                to_diagonal(k - 1)

        def last():
            if line > 1:
                to_diagonal(line - 1)

        def finish():
            for k in range(line):
                panel = panel_at(flip(z, k), flip(face, 3))
                for way in range(2):
                    slot = (which, way, k)
                    arrived(
                        held.at[panel, halves[1 - way]], half_send.at[slot], half_recv.at[slot], face_to[way + 1]
                    )

        steps = [begin, own_diagonal]
        steps += [functools.partial(middle, k) for k in range(1, line)]
        steps += [last, finish]
        return steps

    def block_product(held, a):
        left = jnp.concatenate([values_ref[t, a] for t in range(rounds)], axis=1)
        right = jnp.concatenate([held[columns_ref[0, a, t]] for t in range(rounds)], axis=0)
        return jnp.dot(left, right, preferred_element_type=jnp.float32)

    def panel_start(which, held):
        for k in range(1, n_rep):
            part_out[which, k - 1] = block_product(held, rep_ids[k])
            sends.start(
                part_out.at[which, k - 1], part_in.at[which, k - 1],
                part_send.at[which, k - 1], part_recv.at[which, k - 1], rep_to[k],
            )
        return block_product(held, rep)

    def panel_end(which, total):
        for k in range(1, n_rep):
            arrived(
                part_in.at[which, k - 1], part_send.at[which, k - 1],
                part_recv.at[which, k - 1], rep_to[k],
            )
            total = total + part_in[which, k - 1]
        return total.astype(jnp.bfloat16)

    for step in gather(0, panels):
        step()
    for copy in local[1:]:
        copy.wait()
    hidden = panel_end(0, panel_start(0, panels))

    weight = weight_ref[...]
    pre_act = jnp.dot(hidden, weight, preferred_element_type=jnp.float32)
    grad_pre = (cotangent_ref[...].astype(jnp.float32) * silu_slope(pre_act)).astype(jnp.bfloat16)
    grad_panels[dom] = lax.dot_general(
        grad_pre, weight, (((1,), (1,)), ((), ())), preferred_element_type=jnp.float32
    ).astype(jnp.bfloat16)
    back = gather(1, grad_panels)
    back[0]()

    wide = weight.shape[0]
    rep_rows = wide // n_rep
    line_rows = rep_rows // line
    face_rows, face_columns = line_rows // 2, wide // 2
    rep_base = rep * rep_rows
    line_base = rep_base + z * line_rows
    sem_at = [0]

    def weight_sems(count):
        base = sem_at[0]
        sem_at[0] += count - 1
        return [(weight_send.at[base + k - 1], weight_recv.at[base + k - 1]) for k in range(1, count)]

    def span(start, size):
        return (pl.ds(pl.multiple_of(start, SUBLANES), size),)

    def tile(start, f):
        return (
            pl.ds(pl.multiple_of(start + (f // 2) * face_rows, SUBLANES), face_rows),
            pl.ds(pl.multiple_of((f % 2) * face_columns, LANES), face_columns),
        )

    def exchange(out_ref, in_ref, targets, pieces):
        sems = weight_sems(len(targets))
        for k in range(1, len(targets)):
            sends.start(out_ref.at[pieces[k]], in_ref.at[k - 1], *sems[k - 1], targets[k])
        return sems

    def take(in_ref, sems, targets, total):
        for k in range(1, len(targets)):
            arrived(in_ref.at[k - 1], *sems[k - 1], targets[k])
            total = total + in_ref[k - 1]
        return total

    def share(piece, targets):
        sems = weight_sems(len(targets))
        for k in range(1, len(targets)):
            sends.start(weight_out.at[piece], weight_out.at[piece], *sems[k - 1], targets[k])
        return sems

    def collect(pieces, sems, targets):
        for k in range(1, len(targets)):
            arrived(weight_out.at[pieces[k]], *sems[k - 1], targets[k])

    line_z = [flip(z, k) for k in range(line)]
    face_f = [flip(face, j) for j in range(FACE)]

    weight_part[...] = lax.dot_general(
        hidden, grad_pre, (((0,), (0,)), ((), ())), preferred_element_type=jnp.float32
    )
    sems1 = exchange(weight_part, weight_in1, rep_to, [span(i * rep_rows, rep_rows) for i in rep_ids])
    back[1]()
    back[2]()
    weight_sum1[...] = take(weight_in1, sems1, rep_to, weight_part[span(rep_base, rep_rows)])
    sems2 = exchange(weight_sum1, weight_in2, line_to, [span(i * line_rows, line_rows) for i in line_z])
    for step in back[3:-2]:
        step()
    weight_sum2[...] = take(weight_in2, sems2, line_to, weight_sum1[span(z * line_rows, line_rows)])
    sems3 = exchange(weight_sum2, weight_in3, face_to, [tile(0, f) for f in face_f])
    back[-2]()
    own_sum = take(weight_in3, sems3, face_to, weight_sum2[tile(0, face)])
    weight_out[tile(line_base, face)] = (own_sum * inv_scale).astype(jnp.bfloat16)
    sems4 = share(tile(line_base, face), face_to)
    back[-1]()
    collect([tile(line_base, f) for f in face_f], sems4, face_to)
    sems5 = share(span(line_base, line_rows), line_to)

    total = panel_start(1, grad_panels)
    collect([span(rep_base + i * line_rows, line_rows) for i in line_z], sems5, line_to)
    sems6 = share(span(rep_base, rep_rows), rep_to)
    feature_grad_ref[...] = panel_end(1, total)
    collect([span(i * rep_rows, rep_rows) for i in from_rep_ids], sems6, rep_to)
    weight_grad_ref[...] = weight_out[...]
    sends.finish()


def kernel_shards(features, block_values, block_columns, weight, cotangent):
    n_dom, n_rep = lax.axis_size("dom"), lax.axis_size("rep")
    rows, width = features.shape
    wide = weight.shape[0]
    line = n_dom // FACE
    rep_rows = wide // n_rep
    line_rows = rep_rows // line
    inv_scale = 1.0 / math.sqrt(rows * n_dom * n_rep)
    weight_copies = 2 * ((n_rep - 1) + (line - 1) + (FACE - 1))
    parts, steps = max(n_rep - 1, 1), max(line - 1, 1)
    vmem = pl.BlockSpec(memory_space=pltpu.VMEM)
    any_space = pl.BlockSpec(memory_space=pl.ANY)
    dma = pltpu.SemaphoreType.DMA
    face_slots = (2, 2, line)
    line_slots = (2, steps)
    feature_grad, weight_grad = pl.pallas_call(
        functools.partial(kernel, n_dom, n_rep, inv_scale),
        out_shape=(
            jax.ShapeDtypeStruct((rows, width), jnp.bfloat16),
            jax.ShapeDtypeStruct(weight.shape, jnp.bfloat16),
        ),
        in_specs=[pl.BlockSpec(memory_space=pltpu.SMEM)] + [any_space] * 4,
        out_specs=(vmem, vmem),
        scratch_shapes=[
            pltpu.VMEM(block_values.shape[1:], jnp.bfloat16),
            pltpu.VMEM(weight.shape, jnp.bfloat16),
            pltpu.VMEM(cotangent.shape, jnp.bfloat16),
            pltpu.VMEM((n_dom, rows, width), jnp.bfloat16),
            pltpu.VMEM((n_dom, rows, width), jnp.bfloat16),
            pltpu.VMEM((2, parts, rows, width), jnp.float32),
            pltpu.VMEM((2, parts, rows, width), jnp.float32),
            pltpu.VMEM(weight.shape, jnp.float32),
            pltpu.VMEM((parts, rep_rows, wide), jnp.float32),
            pltpu.VMEM((rep_rows, wide), jnp.float32),
            pltpu.VMEM((steps, line_rows, wide), jnp.float32),
            pltpu.VMEM((line_rows, wide), jnp.float32),
            pltpu.VMEM((FACE - 1, line_rows // 2, wide // 2), jnp.float32),
            pltpu.VMEM(weight.shape, jnp.bfloat16),
            dma((4,)),
            dma(line_slots), dma(line_slots),
            dma(face_slots), dma(face_slots),
            dma(face_slots), dma(face_slots),
            dma((2, parts)), dma((2, parts)),
            dma((weight_copies,)), dma((weight_copies,)),
        ],
        compiler_params=pltpu.CompilerParams(
            collective_id=0, has_side_effects=True, vmem_limit_bytes=VMEM_BYTES
        ),
    )(jnp.swapaxes(block_columns, 1, 2), features, block_values, weight, cotangent)
    return feature_grad, weight_grad.astype(jnp.float32)


def panel_product(values, columns, gathered, block_rows):
    panel_count = gathered.shape[0] // block_rows
    panels = gathered.reshape(panel_count, block_rows, gathered.shape[1])
    picked = panels[columns]
    summed = jnp.einsum("taij,tajf->aif", values, picked, preferred_element_type=jnp.float32)
    return summed.reshape(-1, summed.shape[-1])


def plain_shards(features, block_values, block_columns, weight, cotangent):
    block_rows = features.shape[0]
    values, columns = block_values[0], block_columns[0]
    gathered = lax.all_gather(features, "dom", axis=0, tiled=True)
    inv_scale = 1.0 / math.sqrt(gathered.shape[0] * lax.axis_size("rep"))
    partial_value = panel_product(values, columns, gathered, block_rows)
    hidden = lax.psum_scatter(partial_value, "rep", scatter_dimension=0, tiled=True).astype(jnp.bfloat16)
    pre_act = jnp.dot(hidden, weight, preferred_element_type=jnp.float32)
    grad_pre = (cotangent.astype(jnp.float32) * silu_slope(pre_act)).astype(jnp.bfloat16)
    hidden_grad = jnp.einsum(
        "rg,fg->rf", grad_pre, weight, preferred_element_type=jnp.float32
    ).astype(jnp.bfloat16)
    weight_part = jnp.einsum("rf,rg->fg", hidden, grad_pre, preferred_element_type=jnp.float32)
    weight_grad = lax.psum(weight_part, ("dom", "rep")) * inv_scale
    grad_rows = lax.all_gather(hidden_grad, "dom", axis=0, tiled=True)
    back_partial = panel_product(values, columns, grad_rows, block_rows)
    feature_grad = lax.psum_scatter(back_partial, "rep", scatter_dimension=0, tiled=True)
    return (feature_grad.astype(jnp.bfloat16), weight_grad)


def shards(features, block_values, block_columns, weight, cotangent):
    n_dom, n_rep = lax.axis_size("dom"), lax.axis_size("rep")
    line = n_dom // FACE
    splits = (
        n_dom % FACE == 0
        and line & (line - 1) == 0
        and weight.shape[0] % (2 * SUBLANES * line * n_rep) == 0
        and weight.shape[0] % (2 * LANES) == 0
        and features.shape[0] % (2 * SUBLANES) == 0
    )
    body = kernel_shards if splits else plain_shards
    return body(features, block_values, block_columns, weight, cotangent)


def solution(mesh):
    return jax.shard_map(
        shards,
        mesh=mesh,
        in_specs=(
            P(("dom", "rep"), None),
            P(("dom", "rep"), None, None, None, None),
            P(("dom", "rep"), None, None),
            P(),
            P(("dom", "rep"), None),
        ),
        out_specs=(P(("dom", "rep"), None), P()),
        check_vma=False,
    )
```

```python
import functools
import math

import jax
import jax.numpy as jnp
from jax import lax
from jax.experimental import pallas as pl
from jax.experimental.pallas import tpu as pltpu
from jax.sharding import PartitionSpec as P

MESH = pl.DeviceIdType.MESH
FACE = 4
SUBLANES = 16
LANES = 128
VMEM_BYTES = 60 * 1024 * 1024


def flip(index, offset):
    result, bit = index, 1
    while bit <= offset:
        if offset & bit:
            result = result + bit - 2 * bit * ((index // bit) % 2)
        bit *= 2
    return result


def silu_slope(pre_act):
    sigmoid_value = jax.nn.sigmoid(pre_act)
    return sigmoid_value * (1.0 + pre_act * (1.0 - sigmoid_value))


class Sends:
    def __init__(self):
        self.started = []

    def start(self, src, dst, send_sem, recv_sem, target):
        copy = pltpu.make_async_remote_copy(
            src_ref=src, dst_ref=dst, send_sem=send_sem, recv_sem=recv_sem,
            device_id=target, device_id_type=MESH,
        )
        copy.start()
        self.started.append(copy)

    def finish(self):
        for copy in self.started:
            copy.wait_send()


def arrived(ref, send_sem, recv_sem, target):
    pltpu.make_async_remote_copy(
        src_ref=ref, dst_ref=ref, send_sem=send_sem, recv_sem=recv_sem,
        device_id=target, device_id_type=MESH,
    ).wait_recv()


def kernel(
    n_dom, n_rep, inv_scale,
    columns_ref, features_hbm, values_hbm, weight_hbm, cotangent_hbm,
    feature_grad_ref, weight_grad_ref,
    values_ref, weight_ref, cotangent_ref, panels, grad_panels, part_out, part_in,
    weight_part, weight_in1, weight_sum1, weight_in2, weight_sum2, weight_in3, weight_out,
    local_sem, line_send, line_recv, full_send, full_recv, half_send, half_recv,
    part_send, part_recv, weight_send, weight_recv,
):
    rows = cotangent_ref.shape[0]
    rounds = values_ref.shape[0]
    line = n_dom // FACE
    dom, rep = lax.axis_index("dom"), lax.axis_index("rep")
    z, face = dom // FACE, dom % FACE

    def panel_at(z_at, face_at):
        return z_at * FACE + face_at

    line_ids = [panel_at(flip(z, k), face) for k in range(line)]
    face_ids = [panel_at(z, flip(face, j)) for j in range(FACE)]
    rep_ids = [lax.rem(rep + k, n_rep) for k in range(n_rep)]
    from_rep_ids = [lax.rem(rep - k + n_rep, n_rep) for k in range(n_rep)]
    line_to = [{"dom": i} for i in line_ids]
    face_to = [{"dom": i} for i in face_ids]
    rep_to = [{"rep": i} for i in rep_ids]

    local = [
        pltpu.make_async_copy(src, dst, local_sem.at[i])
        for i, (src, dst) in enumerate((
            (features_hbm, panels.at[dom]),
            (values_hbm.at[0], values_ref),
            (weight_hbm, weight_ref),
            (cotangent_hbm, cotangent_ref),
        ))
    ]
    for copy in local:
        copy.start()

    barrier = pltpu.get_barrier_semaphore()
    partners = line_to[1:] + face_to[1:] + rep_to[1:]
    for target in partners:
        pl.semaphore_signal(barrier, inc=1, device_id=target, device_id_type=MESH)
    local[0].wait()
    pl.semaphore_wait(barrier, len(partners))

    sends = Sends()
    half = rows // 2

    def gather(which, held):
        halves = (pl.ds(0, half), pl.ds(half, half))

        def along(k):
            own = held.at[dom]
            sends.start(own, own, line_send.at[which, k - 1], line_recv.at[which, k - 1], line_to[k])

        def to_neighbours(k):
            piece = held.at[line_ids[k]]
            for way in range(2):
                slot = (which, way, k)
                sends.start(piece, piece, full_send.at[slot], full_recv.at[slot], face_to[way + 1])

        def to_diagonal(k):
            for way in range(2):
                panel = panel_at(flip(z, k), flip(face, way + 1))
                slot = (which, way, k)
                arrived(held.at[panel], full_send.at[slot], full_recv.at[slot], face_to[way + 1])
                piece = held.at[panel, halves[way]]
                slot = (which, 1 - way, k)
                sends.start(piece, piece, half_send.at[slot], half_recv.at[slot], face_to[2 - way])

        def begin():
            for k in range(1, line):
                along(k)
            to_neighbours(0)

        def own_diagonal():
            to_diagonal(0)

        def middle(k):
            arrived(held.at[line_ids[k]], line_send.at[which, k - 1], line_recv.at[which, k - 1], line_to[k])
            to_neighbours(k)
            if k > 1:
                to_diagonal(k - 1)

        def last():
            if line > 1:
                to_diagonal(line - 1)

        def finish():
            for k in range(line):
                panel = panel_at(flip(z, k), flip(face, 3))
                for way in range(2):
                    slot = (which, way, k)
                    arrived(
                        held.at[panel, halves[1 - way]], half_send.at[slot], half_recv.at[slot], face_to[way + 1]
                    )

        steps = [begin, own_diagonal]
        steps += [functools.partial(middle, k) for k in range(1, line)]
        steps += [last, finish]
        return steps

    def block_product(held, a):
        left = jnp.concatenate([values_ref[t, a] for t in range(rounds)], axis=1)
        right = jnp.concatenate([held[columns_ref[0, a, t]] for t in range(rounds)], axis=0)
        return jnp.dot(left, right, preferred_element_type=jnp.float32)

    def panel_start(which, held):
        for k in range(1, n_rep):
            part_out[which, k - 1] = block_product(held, rep_ids[k])
            sends.start(
                part_out.at[which, k - 1], part_in.at[which, k - 1],
                part_send.at[which, k - 1], part_recv.at[which, k - 1], rep_to[k],
            )
        return block_product(held, rep)

    def panel_end(which, total):
        for k in range(1, n_rep):
            arrived(
                part_in.at[which, k - 1], part_send.at[which, k - 1],
                part_recv.at[which, k - 1], rep_to[k],
            )
            total = total + part_in[which, k - 1]
        return total.astype(jnp.bfloat16)

    for step in gather(0, panels):
        step()
    for copy in local[1:]:
        copy.wait()
    hidden = panel_end(0, panel_start(0, panels))

    weight = weight_ref[...]
    pre_act = jnp.dot(hidden, weight, preferred_element_type=jnp.float32)
    grad_pre = (cotangent_ref[...].astype(jnp.float32) * silu_slope(pre_act)).astype(jnp.bfloat16)
    grad_panels[dom] = lax.dot_general(
        grad_pre, weight, (((1,), (1,)), ((), ())), preferred_element_type=jnp.float32
    ).astype(jnp.bfloat16)
    back = gather(1, grad_panels)
    back[0]()

    wide = weight.shape[0]
    rep_rows = wide // n_rep
    line_rows = rep_rows // line
    face_rows, face_columns = line_rows // 2, wide // 2
    rep_base = rep * rep_rows
    line_base = rep_base + z * line_rows
    sem_at = [0]

    def weight_sems(count):
        base = sem_at[0]
        sem_at[0] += count - 1
        return [(weight_send.at[base + k - 1], weight_recv.at[base + k - 1]) for k in range(1, count)]

    def span(start, size):
        return (pl.ds(pl.multiple_of(start, SUBLANES), size),)

    def tile(start, f):
        return (
            pl.ds(pl.multiple_of(start + (f // 2) * face_rows, SUBLANES), face_rows),
            pl.ds(pl.multiple_of((f % 2) * face_columns, LANES), face_columns),
        )

    def exchange(out_ref, in_ref, targets, pieces):
        sems = weight_sems(len(targets))
        for k in range(1, len(targets)):
            sends.start(out_ref.at[pieces[k]], in_ref.at[k - 1], *sems[k - 1], targets[k])
        return sems

    def take(in_ref, sems, targets, total):
        for k in range(1, len(targets)):
            arrived(in_ref.at[k - 1], *sems[k - 1], targets[k])
            total = total + in_ref[k - 1]
        return total

    def share(piece, targets):
        sems = weight_sems(len(targets))
        for k in range(1, len(targets)):
            sends.start(weight_out.at[piece], weight_out.at[piece], *sems[k - 1], targets[k])
        return sems

    def collect(pieces, sems, targets):
        for k in range(1, len(targets)):
            arrived(weight_out.at[pieces[k]], *sems[k - 1], targets[k])

    line_z = [flip(z, k) for k in range(line)]
    face_f = [flip(face, j) for j in range(FACE)]

    weight_part[...] = lax.dot_general(
        hidden, grad_pre, (((0,), (0,)), ((), ())), preferred_element_type=jnp.float32
    )
    sems1 = exchange(weight_part, weight_in1, rep_to, [span(i * rep_rows, rep_rows) for i in rep_ids])
    back[1]()
    back[2]()
    weight_sum1[...] = take(weight_in1, sems1, rep_to, weight_part[span(rep_base, rep_rows)])
    sems2 = exchange(weight_sum1, weight_in2, line_to, [span(i * line_rows, line_rows) for i in line_z])
    for step in back[3:-2]:
        step()
    weight_sum2[...] = take(weight_in2, sems2, line_to, weight_sum1[span(z * line_rows, line_rows)])
    sems3 = exchange(weight_sum2, weight_in3, face_to, [tile(0, f) for f in face_f])
    back[-2]()
    own_sum = take(weight_in3, sems3, face_to, weight_sum2[tile(0, face)])
    weight_out[tile(line_base, face)] = (own_sum * inv_scale).astype(jnp.bfloat16)
    sems4 = share(tile(line_base, face), face_to)
    back[-1]()
    collect([tile(line_base, f) for f in face_f], sems4, face_to)
    sems5 = share(span(line_base, line_rows), line_to)

    total = panel_start(1, grad_panels)
    collect([span(rep_base + i * line_rows, line_rows) for i in line_z], sems5, line_to)
    sems6 = share(span(rep_base, rep_rows), rep_to)
    feature_grad_ref[...] = panel_end(1, total)
    collect([span(i * rep_rows, rep_rows) for i in from_rep_ids], sems6, rep_to)
    weight_grad_ref[...] = weight_out[...].astype(jnp.float32)
    sends.finish()


def kernel_shards(features, block_values, block_columns, weight, cotangent):
    n_dom, n_rep = lax.axis_size("dom"), lax.axis_size("rep")
    rows, width = features.shape
    wide = weight.shape[0]
    line = n_dom // FACE
    rep_rows = wide // n_rep
    line_rows = rep_rows // line
    inv_scale = 1.0 / math.sqrt(rows * n_dom * n_rep)
    weight_copies = 2 * ((n_rep - 1) + (line - 1) + (FACE - 1))
    parts, steps = max(n_rep - 1, 1), max(line - 1, 1)
    vmem = pl.BlockSpec(memory_space=pltpu.VMEM)
    hbm = pl.BlockSpec(memory_space=pl.ANY)
    dma = pltpu.SemaphoreType.DMA
    face_slots = (2, 2, line)
    line_slots = (2, steps)
    return pl.pallas_call(
        functools.partial(kernel, n_dom, n_rep, inv_scale),
        out_shape=(
            jax.ShapeDtypeStruct((rows, width), jnp.bfloat16),
            jax.ShapeDtypeStruct(weight.shape, jnp.float32),
        ),
        in_specs=[pl.BlockSpec(memory_space=pltpu.SMEM)] + [hbm] * 4,
        out_specs=(vmem, vmem),
        scratch_shapes=[
            pltpu.VMEM(block_values.shape[1:], jnp.bfloat16),
            pltpu.VMEM(weight.shape, jnp.bfloat16),
            pltpu.VMEM(cotangent.shape, jnp.bfloat16),
            pltpu.VMEM((n_dom, rows, width), jnp.bfloat16),
            pltpu.VMEM((n_dom, rows, width), jnp.bfloat16),
            pltpu.VMEM((2, parts, rows, width), jnp.float32),
            pltpu.VMEM((2, parts, rows, width), jnp.float32),
            pltpu.VMEM(weight.shape, jnp.float32),
            pltpu.VMEM((parts, rep_rows, wide), jnp.float32),
            pltpu.VMEM((rep_rows, wide), jnp.float32),
            pltpu.VMEM((steps, line_rows, wide), jnp.float32),
            pltpu.VMEM((line_rows, wide), jnp.float32),
            pltpu.VMEM((FACE - 1, line_rows // 2, wide // 2), jnp.float32),
            pltpu.VMEM(weight.shape, jnp.bfloat16),
            dma((4,)),
            dma(line_slots), dma(line_slots),
            dma(face_slots), dma(face_slots),
            dma(face_slots), dma(face_slots),
            dma((2, parts)), dma((2, parts)),
            dma((weight_copies,)), dma((weight_copies,)),
        ],
        compiler_params=pltpu.CompilerParams(
            collective_id=0, has_side_effects=True, vmem_limit_bytes=VMEM_BYTES
        ),
    )(jnp.swapaxes(block_columns, 1, 2), features, block_values, weight, cotangent)


def panel_product(values, columns, gathered, block_rows):
    panel_count = gathered.shape[0] // block_rows
    panels = gathered.reshape(panel_count, block_rows, gathered.shape[1])
    picked = panels[columns]
    summed = jnp.einsum("taij,tajf->aif", values, picked, preferred_element_type=jnp.float32)
    return summed.reshape(-1, summed.shape[-1])


def plain_shards(features, block_values, block_columns, weight, cotangent):
    block_rows = features.shape[0]
    values, columns = block_values[0], block_columns[0]
    gathered = lax.all_gather(features, "dom", axis=0, tiled=True)
    inv_scale = 1.0 / math.sqrt(gathered.shape[0] * lax.axis_size("rep"))
    partial_value = panel_product(values, columns, gathered, block_rows)
    hidden = lax.psum_scatter(partial_value, "rep", scatter_dimension=0, tiled=True).astype(jnp.bfloat16)
    pre_act = jnp.dot(hidden, weight, preferred_element_type=jnp.float32)
    grad_pre = (cotangent.astype(jnp.float32) * silu_slope(pre_act)).astype(jnp.bfloat16)
    hidden_grad = jnp.einsum(
        "rg,fg->rf", grad_pre, weight, preferred_element_type=jnp.float32
    ).astype(jnp.bfloat16)
    weight_part = jnp.einsum("rf,rg->fg", hidden, grad_pre, preferred_element_type=jnp.float32)
    weight_grad = lax.psum(weight_part, ("dom", "rep")) * inv_scale
    grad_rows = lax.all_gather(hidden_grad, "dom", axis=0, tiled=True)
    back_partial = panel_product(values, columns, grad_rows, block_rows)
    feature_grad = lax.psum_scatter(back_partial, "rep", scatter_dimension=0, tiled=True)
    return (feature_grad.astype(jnp.bfloat16), weight_grad)


def shards(features, block_values, block_columns, weight, cotangent):
    n_dom, n_rep = lax.axis_size("dom"), lax.axis_size("rep")
    line = n_dom // FACE
    splits = (
        n_dom % FACE == 0
        and line & (line - 1) == 0
        and weight.shape[0] % (2 * SUBLANES * line * n_rep) == 0
        and weight.shape[0] % (2 * LANES) == 0
        and features.shape[0] % (2 * SUBLANES) == 0
    )
    body = kernel_shards if splits else plain_shards
    return body(features, block_values, block_columns, weight, cotangent)


def solution(mesh):
    return jax.shard_map(
        shards,
        mesh=mesh,
        in_specs=(
            P(("dom", "rep"), None),
            P(("dom", "rep"), None, None, None, None),
            P(("dom", "rep"), None, None),
            P(),
            P(("dom", "rep"), None),
        ),
        out_specs=(P(("dom", "rep"), None), P()),
        check_vma=False,
    )
```

```python
import functools
import math

import jax
import jax.numpy as jnp
from jax import lax
from jax.experimental import pallas as pl
from jax.experimental.pallas import tpu as pltpu
from jax.sharding import PartitionSpec as P

MESH = pl.DeviceIdType.MESH
FACE = 4
SUBLANES = 16
LANES = 128
VMEM_BYTES = 60 * 1024 * 1024


def flip(index, offset):
    result, bit = index, 1
    while bit <= offset:
        if offset & bit:
            result = result + bit - 2 * bit * ((index // bit) % 2)
        bit *= 2
    return result


def silu_slope(pre_act):
    sigmoid_value = jax.nn.sigmoid(pre_act)
    return sigmoid_value * (1.0 + pre_act * (1.0 - sigmoid_value))


class Sends:
    def __init__(self):
        self.started = []

    def start(self, src, dst, send_sem, recv_sem, target):
        copy = pltpu.make_async_remote_copy(
            src_ref=src, dst_ref=dst, send_sem=send_sem, recv_sem=recv_sem,
            device_id=target, device_id_type=MESH,
        )
        copy.start()
        self.started.append(copy)

    def finish(self):
        for copy in self.started:
            copy.wait_send()


def arrived(ref, send_sem, recv_sem, target):
    pltpu.make_async_remote_copy(
        src_ref=ref, dst_ref=ref, send_sem=send_sem, recv_sem=recv_sem,
        device_id=target, device_id_type=MESH,
    ).wait_recv()


def kernel(
    n_dom, n_rep, inv_scale,
    columns_ref, features_hbm, values_hbm, weight_hbm, cotangent_hbm,
    feature_grad_ref, weight_grad_ref,
    values_ref, weight_ref, cotangent_ref, panels, grad_panels, part_out, part_in,
    weight_part, weight_in1, weight_sum1, weight_in2, weight_sum2, weight_in3, weight_out,
    local_sem, line_send, line_recv, full_send, full_recv, half_send, half_recv,
    part_send, part_recv, weight_send, weight_recv,
):
    rows = cotangent_ref.shape[0]
    rounds = values_ref.shape[0]
    line = n_dom // FACE
    dom, rep = lax.axis_index("dom"), lax.axis_index("rep")
    z, face = dom // FACE, dom % FACE

    def panel_at(z_at, face_at):
        return z_at * FACE + face_at

    line_ids = [panel_at(flip(z, k), face) for k in range(line)]
    face_ids = [panel_at(z, flip(face, j)) for j in range(FACE)]
    rep_ids = [lax.rem(rep + k, n_rep) for k in range(n_rep)]
    from_rep_ids = [lax.rem(rep - k + n_rep, n_rep) for k in range(n_rep)]
    line_to = [{"dom": i} for i in line_ids]
    face_to = [{"dom": i} for i in face_ids]
    rep_to = [{"rep": i} for i in rep_ids]

    local = [
        pltpu.make_async_copy(src, dst, local_sem.at[i])
        for i, (src, dst) in enumerate((
            (features_hbm, panels.at[dom]),
            (values_hbm.at[0], values_ref),
            (weight_hbm, weight_ref),
            (cotangent_hbm, cotangent_ref),
        ))
    ]
    for copy in local:
        copy.start()

    barrier = pltpu.get_barrier_semaphore()
    partners = line_to[1:] + face_to[1:] + rep_to[1:]
    for target in partners:
        pl.semaphore_signal(barrier, inc=1, device_id=target, device_id_type=MESH)
    local[0].wait()
    pl.semaphore_wait(barrier, len(partners))

    sends = Sends()
    half = rows // 2

    def gather(which, held):
        halves = (pl.ds(0, half), pl.ds(half, half))

        def along(k):
            own = held.at[dom]
            sends.start(own, own, line_send.at[which, k - 1], line_recv.at[which, k - 1], line_to[k])

        def to_neighbours(k):
            piece = held.at[line_ids[k]]
            for way in range(2):
                slot = (which, way, k)
                sends.start(piece, piece, full_send.at[slot], full_recv.at[slot], face_to[way + 1])

        def to_diagonal(k):
            for way in range(2):
                panel = panel_at(flip(z, k), flip(face, way + 1))
                slot = (which, way, k)
                arrived(held.at[panel], full_send.at[slot], full_recv.at[slot], face_to[way + 1])
                piece = held.at[panel, halves[way]]
                slot = (which, 1 - way, k)
                sends.start(piece, piece, half_send.at[slot], half_recv.at[slot], face_to[2 - way])

        def begin():
            for k in range(1, line):
                along(k)
            to_neighbours(0)

        def own_diagonal():
            to_diagonal(0)

        def middle(k):
            arrived(held.at[line_ids[k]], line_send.at[which, k - 1], line_recv.at[which, k - 1], line_to[k])
            to_neighbours(k)
            if k > 1:
                to_diagonal(k - 1)

        def last():
            if line > 1:
                to_diagonal(line - 1)

        def finish():
            for k in range(line):
                panel = panel_at(flip(z, k), flip(face, 3))
                for way in range(2):
                    slot = (which, way, k)
                    arrived(
                        held.at[panel, halves[1 - way]], half_send.at[slot], half_recv.at[slot], face_to[way + 1]
                    )

        steps = [begin, own_diagonal]
        steps += [functools.partial(middle, k) for k in range(1, line)]
        steps += [last, finish]
        return steps

    def block_product(held, a):
        left = jnp.concatenate([values_ref[t, a] for t in range(rounds)], axis=1)
        right = jnp.concatenate([held[columns_ref[0, a, t]] for t in range(rounds)], axis=0)
        return jnp.dot(left, right, preferred_element_type=jnp.float32)

    def panel_start(which, held):
        for k in range(1, n_rep):
            part_out[which, k - 1] = block_product(held, rep_ids[k])
            sends.start(
                part_out.at[which, k - 1], part_in.at[which, k - 1],
                part_send.at[which, k - 1], part_recv.at[which, k - 1], rep_to[k],
            )
        return block_product(held, rep)

    def panel_end(which, total):
        for k in range(1, n_rep):
            arrived(
                part_in.at[which, k - 1], part_send.at[which, k - 1],
                part_recv.at[which, k - 1], rep_to[k],
            )
            total = total + part_in[which, k - 1]
        return total.astype(jnp.bfloat16)

    for step in gather(0, panels):
        step()
    for copy in local[1:]:
        copy.wait()
    hidden = panel_end(0, panel_start(0, panels))

    weight = weight_ref[...]
    pre_act = jnp.dot(hidden, weight, preferred_element_type=jnp.float32)
    grad_pre = (cotangent_ref[...].astype(jnp.float32) * silu_slope(pre_act)).astype(jnp.bfloat16)
    grad_panels[dom] = lax.dot_general(
        grad_pre, weight, (((1,), (1,)), ((), ())), preferred_element_type=jnp.float32
    ).astype(jnp.bfloat16)
    back = gather(1, grad_panels)
    back[0]()

    wide = weight.shape[0]
    rep_rows = wide // n_rep
    face_rows = rep_rows // FACE
    line_rows, line_columns = 2 * face_rows // line, wide // 2
    rep_base = rep * rep_rows
    face_base = rep_base + face * face_rows
    sem_at = [0]

    def weight_sems(count):
        base = sem_at[0]
        sem_at[0] += count - 1
        return [(weight_send.at[base + k - 1], weight_recv.at[base + k - 1]) for k in range(1, count)]

    def span(start, size):
        return (pl.ds(pl.multiple_of(start, SUBLANES), size),)

    def tile(start, z_at):
        return (
            pl.ds(pl.multiple_of(start + (z_at // 2) * line_rows, SUBLANES), line_rows),
            pl.ds(pl.multiple_of((z_at % 2) * line_columns, LANES), line_columns),
        )

    def exchange(out_ref, in_ref, targets, pieces):
        sems = weight_sems(len(targets))
        for k in range(1, len(targets)):
            sends.start(out_ref.at[pieces[k]], in_ref.at[k - 1], *sems[k - 1], targets[k])
        return sems

    def take(in_ref, sems, targets, total):
        for k in range(1, len(targets)):
            arrived(in_ref.at[k - 1], *sems[k - 1], targets[k])
            total = total + in_ref[k - 1]
        return total

    def share(piece, targets):
        sems = weight_sems(len(targets))
        for k in range(1, len(targets)):
            sends.start(weight_out.at[piece], weight_out.at[piece], *sems[k - 1], targets[k])
        return sems

    def collect(pieces, sems, targets):
        for k in range(1, len(targets)):
            arrived(weight_out.at[pieces[k]], *sems[k - 1], targets[k])

    line_z = [flip(z, k) for k in range(line)]
    face_f = [flip(face, j) for j in range(FACE)]

    weight_part[...] = lax.dot_general(
        hidden, grad_pre, (((0,), (0,)), ((), ())), preferred_element_type=jnp.float32
    )
    sems1 = exchange(weight_part, weight_in1, rep_to, [span(i * rep_rows, rep_rows) for i in rep_ids])
    back[1]()
    weight_sum1[...] = take(weight_in1, sems1, rep_to, weight_part[span(rep_base, rep_rows)])
    sems2 = exchange(weight_sum1, weight_in2, face_to, [span(f * face_rows, face_rows) for f in face_f])
    for step in back[2:3]:
        step()
    weight_sum2[...] = take(weight_in2, sems2, face_to, weight_sum1[span(face * face_rows, face_rows)])
    sems3 = exchange(weight_sum2, weight_in3, line_to, [tile(0, i) for i in line_z])
    for step in back[3:-2]:
        step()
    own_sum = take(weight_in3, sems3, line_to, weight_sum2[tile(0, z)])
    weight_out[tile(face_base, z)] = (own_sum * inv_scale).astype(jnp.bfloat16)
    sems4 = share(tile(face_base, z), line_to)
    back[-2]()
    collect([tile(face_base, i) for i in line_z], sems4, line_to)
    sems5 = share(span(face_base, face_rows), face_to)
    back[-1]()

    total = panel_start(1, grad_panels)
    collect([span(rep_base + f * face_rows, face_rows) for f in face_f], sems5, face_to)
    sems6 = share(span(rep_base, rep_rows), rep_to)
    feature_grad_ref[...] = panel_end(1, total)
    collect([span(i * rep_rows, rep_rows) for i in from_rep_ids], sems6, rep_to)
    weight_grad_ref[...] = weight_out[...].astype(jnp.float32)
    sends.finish()


def kernel_shards(features, block_values, block_columns, weight, cotangent):
    n_dom, n_rep = lax.axis_size("dom"), lax.axis_size("rep")
    rows, width = features.shape
    wide = weight.shape[0]
    line = n_dom // FACE
    rep_rows = wide // n_rep
    face_rows = rep_rows // FACE
    inv_scale = 1.0 / math.sqrt(rows * n_dom * n_rep)
    weight_copies = 2 * ((n_rep - 1) + (line - 1) + (FACE - 1))
    parts, steps = max(n_rep - 1, 1), max(line - 1, 1)
    vmem = pl.BlockSpec(memory_space=pltpu.VMEM)
    hbm = pl.BlockSpec(memory_space=pl.ANY)
    dma = pltpu.SemaphoreType.DMA
    face_slots = (2, 2, line)
    line_slots = (2, steps)
    return pl.pallas_call(
        functools.partial(kernel, n_dom, n_rep, inv_scale),
        out_shape=(
            jax.ShapeDtypeStruct((rows, width), jnp.bfloat16),
            jax.ShapeDtypeStruct(weight.shape, jnp.float32),
        ),
        in_specs=[pl.BlockSpec(memory_space=pltpu.SMEM)] + [hbm] * 4,
        out_specs=(vmem, vmem),
        scratch_shapes=[
            pltpu.VMEM(block_values.shape[1:], jnp.bfloat16),
            pltpu.VMEM(weight.shape, jnp.bfloat16),
            pltpu.VMEM(cotangent.shape, jnp.bfloat16),
            pltpu.VMEM((n_dom, rows, width), jnp.bfloat16),
            pltpu.VMEM((n_dom, rows, width), jnp.bfloat16),
            pltpu.VMEM((2, parts, rows, width), jnp.float32),
            pltpu.VMEM((2, parts, rows, width), jnp.float32),
            pltpu.VMEM(weight.shape, jnp.float32),
            pltpu.VMEM((parts, rep_rows, wide), jnp.float32),
            pltpu.VMEM((rep_rows, wide), jnp.float32),
            pltpu.VMEM((FACE - 1, face_rows, wide), jnp.float32),
            pltpu.VMEM((face_rows, wide), jnp.float32),
            pltpu.VMEM((steps, 2 * face_rows // line, wide // 2), jnp.float32),
            pltpu.VMEM(weight.shape, jnp.bfloat16),
            dma((4,)),
            dma(line_slots), dma(line_slots),
            dma(face_slots), dma(face_slots),
            dma(face_slots), dma(face_slots),
            dma((2, parts)), dma((2, parts)),
            dma((weight_copies,)), dma((weight_copies,)),
        ],
        compiler_params=pltpu.CompilerParams(
            collective_id=0, has_side_effects=True, vmem_limit_bytes=VMEM_BYTES
        ),
    )(jnp.swapaxes(block_columns, 1, 2), features, block_values, weight, cotangent)


def panel_product(values, columns, gathered, block_rows):
    panel_count = gathered.shape[0] // block_rows
    panels = gathered.reshape(panel_count, block_rows, gathered.shape[1])
    picked = panels[columns]
    summed = jnp.einsum("taij,tajf->aif", values, picked, preferred_element_type=jnp.float32)
    return summed.reshape(-1, summed.shape[-1])


def plain_shards(features, block_values, block_columns, weight, cotangent):
    block_rows = features.shape[0]
    values, columns = block_values[0], block_columns[0]
    gathered = lax.all_gather(features, "dom", axis=0, tiled=True)
    inv_scale = 1.0 / math.sqrt(gathered.shape[0] * lax.axis_size("rep"))
    partial_value = panel_product(values, columns, gathered, block_rows)
    hidden = lax.psum_scatter(partial_value, "rep", scatter_dimension=0, tiled=True).astype(jnp.bfloat16)
    pre_act = jnp.dot(hidden, weight, preferred_element_type=jnp.float32)
    grad_pre = (cotangent.astype(jnp.float32) * silu_slope(pre_act)).astype(jnp.bfloat16)
    hidden_grad = jnp.einsum(
        "rg,fg->rf", grad_pre, weight, preferred_element_type=jnp.float32
    ).astype(jnp.bfloat16)
    weight_part = jnp.einsum("rf,rg->fg", hidden, grad_pre, preferred_element_type=jnp.float32)
    weight_grad = lax.psum(weight_part, ("dom", "rep")) * inv_scale
    grad_rows = lax.all_gather(hidden_grad, "dom", axis=0, tiled=True)
    back_partial = panel_product(values, columns, grad_rows, block_rows)
    feature_grad = lax.psum_scatter(back_partial, "rep", scatter_dimension=0, tiled=True)
    return (feature_grad.astype(jnp.bfloat16), weight_grad)


def shards(features, block_values, block_columns, weight, cotangent):
    n_dom, n_rep = lax.axis_size("dom"), lax.axis_size("rep")
    line = n_dom // FACE
    splits = (
        n_dom % FACE == 0
        and line & (line - 1) == 0
        and line > 1
        and weight.shape[0] % (2 * SUBLANES * line * n_rep) == 0
        and weight.shape[0] % (2 * LANES) == 0
        and features.shape[0] % (2 * SUBLANES) == 0
    )
    body = kernel_shards if splits else plain_shards
    return body(features, block_values, block_columns, weight, cotangent)


def solution(mesh):
    return jax.shard_map(
        shards,
        mesh=mesh,
        in_specs=(
            P(("dom", "rep"), None),
            P(("dom", "rep"), None, None, None, None),
            P(("dom", "rep"), None, None),
            P(),
            P(("dom", "rep"), None),
        ),
        out_specs=(P(("dom", "rep"), None), P()),
        check_vma=False,
    )
```

```python
import functools
import math

import jax
import jax.numpy as jnp
from jax import lax
from jax.experimental import pallas as pl
from jax.experimental.pallas import tpu as pltpu
from jax.sharding import PartitionSpec as P

MESH = pl.DeviceIdType.MESH
FACE = 4
SUBLANES = 16
LANES = 128
VMEM_BYTES = 60 * 1024 * 1024


def flip(index, offset):
    result, bit = index, 1
    while bit <= offset:
        if offset & bit:
            result = result + bit - 2 * bit * ((index // bit) % 2)
        bit *= 2
    return result


def silu_slope(pre_act):
    sigmoid_value = jax.nn.sigmoid(pre_act)
    return sigmoid_value * (1.0 + pre_act * (1.0 - sigmoid_value))


class Sends:
    def __init__(self):
        self.started = []

    def start(self, src, dst, send_sem, recv_sem, target):
        copy = pltpu.make_async_remote_copy(
            src_ref=src, dst_ref=dst, send_sem=send_sem, recv_sem=recv_sem,
            device_id=target, device_id_type=MESH,
        )
        copy.start()
        self.started.append(copy)

    def finish(self):
        for copy in self.started:
            copy.wait_send()


def arrived(ref, send_sem, recv_sem, target):
    pltpu.make_async_remote_copy(
        src_ref=ref, dst_ref=ref, send_sem=send_sem, recv_sem=recv_sem,
        device_id=target, device_id_type=MESH,
    ).wait_recv()


def kernel(
    n_dom, n_rep, inv_scale,
    columns_ref, features_hbm, values_hbm, weight_hbm, cotangent_hbm,
    feature_grad_ref, weight_grad_ref,
    values_ref, weight_ref, cotangent_ref, panels, grad_panels, part_out, part_in,
    weight_part, weight_in1, weight_sum1, weight_in2, weight_sum2, weight_in3, weight_out,
    local_sem, line_send, line_recv, full_send, full_recv, half_send, half_recv,
    part_send, part_recv, weight_send, weight_recv,
):
    rows = cotangent_ref.shape[0]
    rounds = values_ref.shape[0]
    line = n_dom // FACE
    dom, rep = lax.axis_index("dom"), lax.axis_index("rep")
    z, face = dom // FACE, dom % FACE

    def panel_at(z_at, face_at):
        return z_at * FACE + face_at

    line_ids = [panel_at(flip(z, k), face) for k in range(line)]
    face_ids = [panel_at(z, flip(face, j)) for j in range(FACE)]
    rep_ids = [lax.rem(rep + k, n_rep) for k in range(n_rep)]
    from_rep_ids = [lax.rem(rep - k + n_rep, n_rep) for k in range(n_rep)]
    line_to = [{"dom": i} for i in line_ids]
    face_to = [{"dom": i} for i in face_ids]
    rep_to = [{"rep": i} for i in rep_ids]

    local = [
        pltpu.make_async_copy(src, dst, local_sem.at[i])
        for i, (src, dst) in enumerate((
            (features_hbm, panels.at[dom]),
            (values_hbm.at[0], values_ref),
            (weight_hbm, weight_ref),
            (cotangent_hbm, cotangent_ref),
        ))
    ]
    for copy in local:
        copy.start()

    barrier = pltpu.get_barrier_semaphore()
    partners = line_to[1:] + face_to[1:] + rep_to[1:]
    for target in partners:
        pl.semaphore_signal(barrier, inc=1, device_id=target, device_id_type=MESH)
    local[0].wait()
    pl.semaphore_wait(barrier, len(partners))

    sends = Sends()
    half = rows // 2

    def gather(which, held):
        halves = (pl.ds(0, half), pl.ds(half, half))

        def along(k):
            own = held.at[dom]
            sends.start(own, own, line_send.at[which, k - 1], line_recv.at[which, k - 1], line_to[k])

        def to_neighbours(k):
            piece = held.at[line_ids[k]]
            for way in range(2):
                slot = (which, way, k)
                sends.start(piece, piece, full_send.at[slot], full_recv.at[slot], face_to[way + 1])

        def to_diagonal(k):
            for way in range(2):
                panel = panel_at(flip(z, k), flip(face, way + 1))
                slot = (which, way, k)
                arrived(held.at[panel], full_send.at[slot], full_recv.at[slot], face_to[way + 1])
                piece = held.at[panel, halves[way]]
                slot = (which, 1 - way, k)
                sends.start(piece, piece, half_send.at[slot], half_recv.at[slot], face_to[2 - way])

        def begin():
            for k in range(1, line):
                along(k)
            to_neighbours(0)

        def own_diagonal():
            to_diagonal(0)

        def middle(k):
            arrived(held.at[line_ids[k]], line_send.at[which, k - 1], line_recv.at[which, k - 1], line_to[k])
            to_neighbours(k)
            if k > 1:
                to_diagonal(k - 1)

        def last():
            if line > 1:
                to_diagonal(line - 1)

        def finish():
            for k in range(line):
                panel = panel_at(flip(z, k), flip(face, 3))
                for way in range(2):
                    slot = (which, way, k)
                    arrived(
                        held.at[panel, halves[1 - way]], half_send.at[slot], half_recv.at[slot], face_to[way + 1]
                    )

        steps = [begin, own_diagonal]
        steps += [functools.partial(middle, k) for k in range(1, line)]
        steps += [last, finish]
        return steps

    def block_product(held, a):
        left = jnp.concatenate([values_ref[t, a] for t in range(rounds)], axis=1)
        right = jnp.concatenate([held[columns_ref[0, a, t]] for t in range(rounds)], axis=0)
        return jnp.dot(left, right, preferred_element_type=jnp.float32)

    def panel_start(which, held):
        for k in range(1, n_rep):
            part_out[which, k - 1] = block_product(held, rep_ids[k])
            sends.start(
                part_out.at[which, k - 1], part_in.at[which, k - 1],
                part_send.at[which, k - 1], part_recv.at[which, k - 1], rep_to[k],
            )
        return block_product(held, rep)

    def panel_end(which, total):
        for k in range(1, n_rep):
            arrived(
                part_in.at[which, k - 1], part_send.at[which, k - 1],
                part_recv.at[which, k - 1], rep_to[k],
            )
            total = total + part_in[which, k - 1]
        return total.astype(jnp.bfloat16)

    for step in gather(0, panels):
        step()
    for copy in local[1:]:
        copy.wait()
    hidden = panel_end(0, panel_start(0, panels))

    weight = weight_ref[...]
    pre_act = jnp.dot(hidden, weight, preferred_element_type=jnp.float32)
    grad_pre = (cotangent_ref[...].astype(jnp.float32) * silu_slope(pre_act)).astype(jnp.bfloat16)
    grad_panels[dom] = lax.dot_general(
        grad_pre, weight, (((1,), (1,)), ((), ())), preferred_element_type=jnp.float32
    ).astype(jnp.bfloat16)
    back = gather(1, grad_panels)
    back[0]()

    wide = weight.shape[0]
    rep_rows = wide // n_rep
    face_rows = rep_rows // FACE
    line_rows, line_columns = 2 * face_rows // line, wide // 2
    rep_base = rep * rep_rows
    face_base = rep_base + face * face_rows
    sem_at = [0]

    def weight_sems(count):
        base = sem_at[0]
        sem_at[0] += count - 1
        return [(weight_send.at[base + k - 1], weight_recv.at[base + k - 1]) for k in range(1, count)]

    def span(start, size):
        return (pl.ds(pl.multiple_of(start, SUBLANES), size),)

    def tile(start, z_at):
        return (
            pl.ds(pl.multiple_of(start + (z_at // 2) * line_rows, SUBLANES), line_rows),
            pl.ds(pl.multiple_of((z_at % 2) * line_columns, LANES), line_columns),
        )

    def exchange(out_ref, in_ref, targets, pieces):
        sems = weight_sems(len(targets))
        for k in range(1, len(targets)):
            sends.start(out_ref.at[pieces[k]], in_ref.at[k - 1], *sems[k - 1], targets[k])
        return sems

    def take(in_ref, sems, targets, total):
        for k in range(1, len(targets)):
            arrived(in_ref.at[k - 1], *sems[k - 1], targets[k])
            total = total + in_ref[k - 1]
        return total

    def share(piece, targets):
        sems = weight_sems(len(targets))
        for k in range(1, len(targets)):
            sends.start(weight_out.at[piece], weight_out.at[piece], *sems[k - 1], targets[k])
        return sems

    def collect(pieces, sems, targets):
        for k in range(1, len(targets)):
            arrived(weight_out.at[pieces[k]], *sems[k - 1], targets[k])

    line_z = [flip(z, k) for k in range(line)]
    face_f = [flip(face, j) for j in range(FACE)]

    weight_part[...] = lax.dot_general(
        hidden, grad_pre, (((0,), (0,)), ((), ())), preferred_element_type=jnp.float32
    )
    sems1 = exchange(weight_part, weight_in1, rep_to, [span(i * rep_rows, rep_rows) for i in rep_ids])
    back[1]()
    weight_sum1[...] = take(weight_in1, sems1, rep_to, weight_part[span(rep_base, rep_rows)])
    sems2 = exchange(weight_sum1, weight_in2, face_to, [span(f * face_rows, face_rows) for f in face_f])
    for step in back[2:3]:
        step()
    weight_sum2[...] = take(weight_in2, sems2, face_to, weight_sum1[span(face * face_rows, face_rows)])
    sems3 = exchange(weight_sum2, weight_in3, line_to, [tile(0, i) for i in line_z])
    for step in back[3:-2]:
        step()
    own_sum = take(weight_in3, sems3, line_to, weight_sum2[tile(0, z)])
    weight_out[tile(face_base, z)] = (own_sum * inv_scale).astype(jnp.bfloat16)
    sems4 = share(tile(face_base, z), line_to)
    back[-2]()
    collect([tile(face_base, i) for i in line_z], sems4, line_to)
    sems5 = share(span(face_base, face_rows), face_to)
    back[-1]()

    total = panel_start(1, grad_panels)
    collect([span(rep_base + f * face_rows, face_rows) for f in face_f], sems5, face_to)
    sems6 = share(span(rep_base, rep_rows), rep_to)
    feature_grad_ref[...] = panel_end(1, total)
    collect([span(i * rep_rows, rep_rows) for i in from_rep_ids], sems6, rep_to)
    weight_grad_ref[...] = weight_out[...].astype(jnp.float32)
    sends.finish()


def kernel_shards(features, block_values, block_columns, weight, cotangent):
    n_dom, n_rep = lax.axis_size("dom"), lax.axis_size("rep")
    rows, width = features.shape
    wide = weight.shape[0]
    line = n_dom // FACE
    rep_rows = wide // n_rep
    face_rows = rep_rows // FACE
    inv_scale = 1.0 / math.sqrt(rows * n_dom * n_rep)
    weight_copies = 2 * ((n_rep - 1) + (line - 1) + (FACE - 1))
    parts, steps = max(n_rep - 1, 1), max(line - 1, 1)
    vmem = pl.BlockSpec(memory_space=pltpu.VMEM)
    hbm = pl.BlockSpec(memory_space=pl.ANY)
    dma = pltpu.SemaphoreType.DMA
    face_slots = (2, 2, line)
    line_slots = (2, steps)
    return pl.pallas_call(
        functools.partial(kernel, n_dom, n_rep, inv_scale),
        out_shape=(
            pltpu.VMEM((rows, width), jnp.bfloat16),
            pltpu.VMEM(weight.shape, jnp.float32),
        ),
        in_specs=[pl.BlockSpec(memory_space=pltpu.SMEM)] + [hbm] * 4,
        out_specs=(vmem, vmem),
        scratch_shapes=[
            pltpu.VMEM(block_values.shape[1:], jnp.bfloat16),
            pltpu.VMEM(weight.shape, jnp.bfloat16),
            pltpu.VMEM(cotangent.shape, jnp.bfloat16),
            pltpu.VMEM((n_dom, rows, width), jnp.bfloat16),
            pltpu.VMEM((n_dom, rows, width), jnp.bfloat16),
            pltpu.VMEM((2, parts, rows, width), jnp.float32),
            pltpu.VMEM((2, parts, rows, width), jnp.float32),
            pltpu.VMEM(weight.shape, jnp.float32),
            pltpu.VMEM((parts, rep_rows, wide), jnp.float32),
            pltpu.VMEM((rep_rows, wide), jnp.float32),
            pltpu.VMEM((FACE - 1, face_rows, wide), jnp.float32),
            pltpu.VMEM((face_rows, wide), jnp.float32),
            pltpu.VMEM((steps, 2 * face_rows // line, wide // 2), jnp.float32),
            pltpu.VMEM(weight.shape, jnp.bfloat16),
            dma((4,)),
            dma(line_slots), dma(line_slots),
            dma(face_slots), dma(face_slots),
            dma(face_slots), dma(face_slots),
            dma((2, parts)), dma((2, parts)),
            dma((weight_copies,)), dma((weight_copies,)),
        ],
        compiler_params=pltpu.CompilerParams(
            collective_id=0, has_side_effects=True, vmem_limit_bytes=VMEM_BYTES
        ),
    )(jnp.swapaxes(block_columns, 1, 2), features, block_values, weight, cotangent)


def panel_product(values, columns, gathered, block_rows):
    panel_count = gathered.shape[0] // block_rows
    panels = gathered.reshape(panel_count, block_rows, gathered.shape[1])
    picked = panels[columns]
    summed = jnp.einsum("taij,tajf->aif", values, picked, preferred_element_type=jnp.float32)
    return summed.reshape(-1, summed.shape[-1])


def plain_shards(features, block_values, block_columns, weight, cotangent):
    block_rows = features.shape[0]
    values, columns = block_values[0], block_columns[0]
    gathered = lax.all_gather(features, "dom", axis=0, tiled=True)
    inv_scale = 1.0 / math.sqrt(gathered.shape[0] * lax.axis_size("rep"))
    partial_value = panel_product(values, columns, gathered, block_rows)
    hidden = lax.psum_scatter(partial_value, "rep", scatter_dimension=0, tiled=True).astype(jnp.bfloat16)
    pre_act = jnp.dot(hidden, weight, preferred_element_type=jnp.float32)
    grad_pre = (cotangent.astype(jnp.float32) * silu_slope(pre_act)).astype(jnp.bfloat16)
    hidden_grad = jnp.einsum(
        "rg,fg->rf", grad_pre, weight, preferred_element_type=jnp.float32
    ).astype(jnp.bfloat16)
    weight_part = jnp.einsum("rf,rg->fg", hidden, grad_pre, preferred_element_type=jnp.float32)
    weight_grad = lax.psum(weight_part, ("dom", "rep")) * inv_scale
    grad_rows = lax.all_gather(hidden_grad, "dom", axis=0, tiled=True)
    back_partial = panel_product(values, columns, grad_rows, block_rows)
    feature_grad = lax.psum_scatter(back_partial, "rep", scatter_dimension=0, tiled=True)
    return (feature_grad.astype(jnp.bfloat16), weight_grad)


def shards(features, block_values, block_columns, weight, cotangent):
    n_dom, n_rep = lax.axis_size("dom"), lax.axis_size("rep")
    line = n_dom // FACE
    splits = (
        n_dom % FACE == 0
        and line & (line - 1) == 0
        and line > 1
        and weight.shape[0] % (2 * SUBLANES * line * n_rep) == 0
        and weight.shape[0] % (2 * LANES) == 0
        and features.shape[0] % (2 * SUBLANES) == 0
    )
    body = kernel_shards if splits else plain_shards
    return body(features, block_values, block_columns, weight, cotangent)


def solution(mesh):
    return jax.shard_map(
        shards,
        mesh=mesh,
        in_specs=(
            P(("dom", "rep"), None),
            P(("dom", "rep"), None, None, None, None),
            P(("dom", "rep"), None, None),
            P(),
            P(("dom", "rep"), None),
        ),
        out_specs=(P(("dom", "rep"), None), P()),
        check_vma=False,
    )
```

```python
import functools
import math

import jax
import jax.numpy as jnp
from jax import lax
from jax.experimental import pallas as pl
from jax.experimental.pallas import tpu as pltpu
from jax.sharding import PartitionSpec as P

MESH = pl.DeviceIdType.MESH
FACE = 4
SUBLANES = 16
LANES = 128
REST = 4
VMEM_BYTES = 60 * 1024 * 1024


def flip(index, offset):
    result, bit = index, 1
    while bit <= offset:
        if offset & bit:
            result = result + bit - 2 * bit * ((index // bit) % 2)
        bit *= 2
    return result


def silu_slope(pre_act):
    sigmoid_value = jax.nn.sigmoid(pre_act)
    return sigmoid_value * (1.0 + pre_act * (1.0 - sigmoid_value))


class Sends:
    def __init__(self):
        self.started = []

    def start(self, src, dst, send_sem, recv_sem, target):
        copy = pltpu.make_async_remote_copy(
            src_ref=src, dst_ref=dst, send_sem=send_sem, recv_sem=recv_sem,
            device_id=target, device_id_type=MESH,
        )
        copy.start()
        self.started.append(copy)

    def finish(self):
        for copy in self.started:
            copy.wait_send()


def arrived(ref, send_sem, recv_sem, target):
    pltpu.make_async_remote_copy(
        src_ref=ref, dst_ref=ref, send_sem=send_sem, recv_sem=recv_sem,
        device_id=target, device_id_type=MESH,
    ).wait_recv()


def kernel(
    n_dom, n_rep, inv_scale,
    columns_ref, features_hbm, values_hbm, weight_hbm, cotangent_hbm,
    feature_grad_ref, weight_grad_ref,
    values_ref, weight_ref, cotangent_ref, panels, grad_panels, part_out, part_in,
    weight_part, weight_in1, weight_sum1, weight_in2, weight_sum2, weight_in3, weight_out,
    local_sem, face_send, face_recv, slab_send, slab_recv, line_send, line_recv, full_send, full_recv, half_send, half_recv,
    part_send, part_recv, weight_send, weight_recv,
):
    rows = cotangent_ref.shape[0]
    rounds = values_ref.shape[0]
    line = n_dom // FACE
    dom, rep = lax.axis_index("dom"), lax.axis_index("rep")
    z, face = dom // FACE, dom % FACE

    def panel_at(z_at, face_at):
        return z_at * FACE + face_at

    line_ids = [panel_at(flip(z, k), face) for k in range(line)]
    face_ids = [panel_at(z, flip(face, j)) for j in range(FACE)]
    rep_ids = [lax.rem(rep + k, n_rep) for k in range(n_rep)]
    from_rep_ids = [lax.rem(rep - k + n_rep, n_rep) for k in range(n_rep)]
    line_to = [{"dom": i} for i in line_ids]
    face_to = [{"dom": i} for i in face_ids]
    rep_to = [{"rep": i} for i in rep_ids]

    local = [
        pltpu.make_async_copy(src, dst, local_sem.at[i])
        for i, (src, dst) in enumerate((
            (features_hbm, panels.at[dom]),
            (values_hbm.at[0], values_ref),
            (weight_hbm, weight_ref),
            (cotangent_hbm, cotangent_ref),
        ))
    ]
    for copy in local:
        copy.start()

    barrier = pltpu.get_barrier_semaphore()
    partners = line_to[1:] + face_to[1:] + rep_to[1:]
    for target in partners:
        pl.semaphore_signal(barrier, inc=1, device_id=target, device_id_type=MESH)
    local[0].wait()
    pl.semaphore_wait(barrier, len(partners))

    sends = Sends()
    most = rows - rows // REST
    half = most // 2

    def gather(which, held):
        main = pl.ds(0, most)
        rest = pl.ds(most, rows - most)
        halves = (pl.ds(0, half), pl.ds(half, half))

        def over_face():
            own = held.at[dom, rest]
            for j in range(1, FACE):
                slot = (which, j - 1)
                sends.start(own, own, face_send.at[slot], face_recv.at[slot], face_to[j])

        def slab_along():
            for j in range(1, FACE):
                slot = (which, j - 1)
                arrived(held.at[face_ids[j], rest], face_send.at[slot], face_recv.at[slot], face_to[j])
            slab = held.at[pl.ds(z * FACE, FACE), rest]
            for k in range(1, line):
                slot = (which, k - 1)
                sends.start(slab, slab, slab_send.at[slot], slab_recv.at[slot], line_to[k])

        def along(k):
            own = held.at[dom, main]
            sends.start(own, own, line_send.at[which, k - 1], line_recv.at[which, k - 1], line_to[k])

        def to_neighbours(k):
            piece = held.at[line_ids[k], main]
            for way in range(2):
                slot = (which, way, k)
                sends.start(piece, piece, full_send.at[slot], full_recv.at[slot], face_to[way + 1])

        def to_diagonal(k):
            for way in range(2):
                panel = panel_at(flip(z, k), flip(face, way + 1))
                slot = (which, way, k)
                arrived(held.at[panel, main], full_send.at[slot], full_recv.at[slot], face_to[way + 1])
                piece = held.at[panel, halves[way]]
                slot = (which, 1 - way, k)
                sends.start(piece, piece, half_send.at[slot], half_recv.at[slot], face_to[2 - way])

        def begin():
            for k in range(1, line):
                along(k)
            over_face()
            to_neighbours(0)

        def own_diagonal():
            to_diagonal(0)

        def middle(k):
            piece = held.at[line_ids[k], main]
            arrived(piece, line_send.at[which, k - 1], line_recv.at[which, k - 1], line_to[k])
            to_neighbours(k)
            if k == line - 1:
                slab_along()
            if k > 1:
                to_diagonal(k - 1)

        def last():
            to_diagonal(line - 1)

        def finish():
            for k in range(line):
                panel = panel_at(flip(z, k), flip(face, 3))
                for way in range(2):
                    slot = (which, way, k)
                    arrived(
                        held.at[panel, halves[1 - way]], half_send.at[slot], half_recv.at[slot], face_to[way + 1]
                    )
            for k in range(1, line):
                slot = (which, k - 1)
                slab = held.at[pl.ds(flip(z, k) * FACE, FACE), rest]
                arrived(slab, slab_send.at[slot], slab_recv.at[slot], line_to[k])

        steps = [begin, own_diagonal]
        steps += [functools.partial(middle, k) for k in range(1, line)]
        steps += [last, finish]
        return steps

    def block_product(held, a):
        left = jnp.concatenate([values_ref[t, a] for t in range(rounds)], axis=1)
        right = jnp.concatenate([held[columns_ref[0, a, t]] for t in range(rounds)], axis=0)
        return jnp.dot(left, right, preferred_element_type=jnp.float32)

    def panel_start(which, held):
        for k in range(1, n_rep):
            part_out[which, k - 1] = block_product(held, rep_ids[k])
            sends.start(
                part_out.at[which, k - 1], part_in.at[which, k - 1],
                part_send.at[which, k - 1], part_recv.at[which, k - 1], rep_to[k],
            )
        return block_product(held, rep)

    def panel_end(which, total):
        for k in range(1, n_rep):
            arrived(
                part_in.at[which, k - 1], part_send.at[which, k - 1],
                part_recv.at[which, k - 1], rep_to[k],
            )
            total = total + part_in[which, k - 1]
        return total.astype(jnp.bfloat16)

    for step in gather(0, panels):
        step()
    for copy in local[1:]:
        copy.wait()
    hidden = panel_end(0, panel_start(0, panels))

    weight = weight_ref[...]
    pre_act = jnp.dot(hidden, weight, preferred_element_type=jnp.float32)
    grad_pre = (cotangent_ref[...].astype(jnp.float32) * silu_slope(pre_act)).astype(jnp.bfloat16)
    grad_panels[dom] = lax.dot_general(
        grad_pre, weight, (((1,), (1,)), ((), ())), preferred_element_type=jnp.float32
    ).astype(jnp.bfloat16)
    back = gather(1, grad_panels)
    back[0]()

    wide = weight.shape[0]
    rep_rows = wide // n_rep
    face_rows = rep_rows // FACE
    line_rows, line_columns = 2 * face_rows // line, wide // 2
    rep_base = rep * rep_rows
    face_base = rep_base + face * face_rows
    sem_at = [0]

    def weight_sems(count):
        base = sem_at[0]
        sem_at[0] += count - 1
        return [(weight_send.at[base + k - 1], weight_recv.at[base + k - 1]) for k in range(1, count)]

    def span(start, size):
        return (pl.ds(pl.multiple_of(start, SUBLANES), size),)

    def tile(start, z_at):
        return (
            pl.ds(pl.multiple_of(start + (z_at // 2) * line_rows, SUBLANES), line_rows),
            pl.ds(pl.multiple_of((z_at % 2) * line_columns, LANES), line_columns),
        )

    def exchange(out_ref, in_ref, targets, pieces):
        sems = weight_sems(len(targets))
        for k in range(1, len(targets)):
            sends.start(out_ref.at[pieces[k]], in_ref.at[k - 1], *sems[k - 1], targets[k])
        return sems

    def take(in_ref, sems, targets, total):
        for k in range(1, len(targets)):
            arrived(in_ref.at[k - 1], *sems[k - 1], targets[k])
            total = total + in_ref[k - 1]
        return total

    def share(piece, targets):
        sems = weight_sems(len(targets))
        for k in range(1, len(targets)):
            sends.start(weight_out.at[piece], weight_out.at[piece], *sems[k - 1], targets[k])
        return sems

    def collect(pieces, sems, targets):
        for k in range(1, len(targets)):
            arrived(weight_out.at[pieces[k]], *sems[k - 1], targets[k])

    line_z = [flip(z, k) for k in range(line)]
    face_f = [flip(face, j) for j in range(FACE)]

    weight_part[...] = lax.dot_general(
        hidden, grad_pre, (((0,), (0,)), ((), ())), preferred_element_type=jnp.float32
    )
    sems1 = exchange(weight_part, weight_in1, rep_to, [span(i * rep_rows, rep_rows) for i in rep_ids])
    back[1]()
    weight_sum1[...] = take(weight_in1, sems1, rep_to, weight_part[span(rep_base, rep_rows)])
    sems2 = exchange(weight_sum1, weight_in2, face_to, [span(f * face_rows, face_rows) for f in face_f])
    for step in back[2:3]:
        step()
    weight_sum2[...] = take(weight_in2, sems2, face_to, weight_sum1[span(face * face_rows, face_rows)])
    sems3 = exchange(weight_sum2, weight_in3, line_to, [tile(0, i) for i in line_z])
    for step in back[3:-2]:
        step()
    own_sum = take(weight_in3, sems3, line_to, weight_sum2[tile(0, z)])
    weight_out[tile(face_base, z)] = (own_sum * inv_scale).astype(jnp.bfloat16)
    sems4 = share(tile(face_base, z), line_to)
    back[-2]()
    collect([tile(face_base, i) for i in line_z], sems4, line_to)
    sems5 = share(span(face_base, face_rows), face_to)
    back[-1]()

    total = panel_start(1, grad_panels)
    collect([span(rep_base + f * face_rows, face_rows) for f in face_f], sems5, face_to)
    sems6 = share(span(rep_base, rep_rows), rep_to)
    feature_grad_ref[...] = panel_end(1, total)
    collect([span(i * rep_rows, rep_rows) for i in from_rep_ids], sems6, rep_to)
    weight_grad_ref[...] = weight_out[...].astype(jnp.float32)
    sends.finish()


def kernel_shards(features, block_values, block_columns, weight, cotangent):
    n_dom, n_rep = lax.axis_size("dom"), lax.axis_size("rep")
    rows, width = features.shape
    wide = weight.shape[0]
    line = n_dom // FACE
    rep_rows = wide // n_rep
    face_rows = rep_rows // FACE
    inv_scale = 1.0 / math.sqrt(rows * n_dom * n_rep)
    weight_copies = 2 * ((n_rep - 1) + (line - 1) + (FACE - 1))
    parts, steps = max(n_rep - 1, 1), max(line - 1, 1)
    vmem = pl.BlockSpec(memory_space=pltpu.VMEM)
    hbm = pl.BlockSpec(memory_space=pl.ANY)
    dma = pltpu.SemaphoreType.DMA
    face_slots = (2, 2, line)
    line_slots = (2, steps)
    return pl.pallas_call(
        functools.partial(kernel, n_dom, n_rep, inv_scale),
        out_shape=(
            pltpu.VMEM((rows, width), jnp.bfloat16),
            pltpu.VMEM(weight.shape, jnp.float32),
        ),
        in_specs=[pl.BlockSpec(memory_space=pltpu.SMEM)] + [hbm] * 4,
        out_specs=(vmem, vmem),
        scratch_shapes=[
            pltpu.VMEM(block_values.shape[1:], jnp.bfloat16),
            pltpu.VMEM(weight.shape, jnp.bfloat16),
            pltpu.VMEM(cotangent.shape, jnp.bfloat16),
            pltpu.VMEM((n_dom, rows, width), jnp.bfloat16),
            pltpu.VMEM((n_dom, rows, width), jnp.bfloat16),
            pltpu.VMEM((2, parts, rows, width), jnp.float32),
            pltpu.VMEM((2, parts, rows, width), jnp.float32),
            pltpu.VMEM(weight.shape, jnp.float32),
            pltpu.VMEM((parts, rep_rows, wide), jnp.float32),
            pltpu.VMEM((rep_rows, wide), jnp.float32),
            pltpu.VMEM((FACE - 1, face_rows, wide), jnp.float32),
            pltpu.VMEM((face_rows, wide), jnp.float32),
            pltpu.VMEM((steps, 2 * face_rows // line, wide // 2), jnp.float32),
            pltpu.VMEM(weight.shape, jnp.bfloat16),
            dma((4,)),
            dma((2, FACE - 1)), dma((2, FACE - 1)),
            dma(line_slots), dma(line_slots),
            dma(line_slots), dma(line_slots),
            dma(face_slots), dma(face_slots),
            dma(face_slots), dma(face_slots),
            dma((2, parts)), dma((2, parts)),
            dma((weight_copies,)), dma((weight_copies,)),
        ],
        compiler_params=pltpu.CompilerParams(
            collective_id=0, has_side_effects=True, vmem_limit_bytes=VMEM_BYTES
        ),
    )(jnp.swapaxes(block_columns, 1, 2), features, block_values, weight, cotangent)


def panel_product(values, columns, gathered, block_rows):
    panel_count = gathered.shape[0] // block_rows
    panels = gathered.reshape(panel_count, block_rows, gathered.shape[1])
    picked = panels[columns]
    summed = jnp.einsum("taij,tajf->aif", values, picked, preferred_element_type=jnp.float32)
    return summed.reshape(-1, summed.shape[-1])


def plain_shards(features, block_values, block_columns, weight, cotangent):
    block_rows = features.shape[0]
    values, columns = block_values[0], block_columns[0]
    gathered = lax.all_gather(features, "dom", axis=0, tiled=True)
    inv_scale = 1.0 / math.sqrt(gathered.shape[0] * lax.axis_size("rep"))
    partial_value = panel_product(values, columns, gathered, block_rows)
    hidden = lax.psum_scatter(partial_value, "rep", scatter_dimension=0, tiled=True).astype(jnp.bfloat16)
    pre_act = jnp.dot(hidden, weight, preferred_element_type=jnp.float32)
    grad_pre = (cotangent.astype(jnp.float32) * silu_slope(pre_act)).astype(jnp.bfloat16)
    hidden_grad = jnp.einsum(
        "rg,fg->rf", grad_pre, weight, preferred_element_type=jnp.float32
    ).astype(jnp.bfloat16)
    weight_part = jnp.einsum("rf,rg->fg", hidden, grad_pre, preferred_element_type=jnp.float32)
    weight_grad = lax.psum(weight_part, ("dom", "rep")) * inv_scale
    grad_rows = lax.all_gather(hidden_grad, "dom", axis=0, tiled=True)
    back_partial = panel_product(values, columns, grad_rows, block_rows)
    feature_grad = lax.psum_scatter(back_partial, "rep", scatter_dimension=0, tiled=True)
    return (feature_grad.astype(jnp.bfloat16), weight_grad)


def shards(features, block_values, block_columns, weight, cotangent):
    n_dom, n_rep = lax.axis_size("dom"), lax.axis_size("rep")
    line = n_dom // FACE
    splits = (
        n_dom % FACE == 0
        and line & (line - 1) == 0
        and line > 1
        and weight.shape[0] % (2 * SUBLANES * line * n_rep) == 0
        and weight.shape[0] % (2 * LANES) == 0
        and features.shape[0] % (2 * SUBLANES * REST) == 0
    )
    body = kernel_shards if splits else plain_shards
    return body(features, block_values, block_columns, weight, cotangent)


def solution(mesh):
    return jax.shard_map(
        shards,
        mesh=mesh,
        in_specs=(
            P(("dom", "rep"), None),
            P(("dom", "rep"), None, None, None, None),
            P(("dom", "rep"), None, None),
            P(),
            P(("dom", "rep"), None),
        ),
        out_specs=(P(("dom", "rep"), None), P()),
        check_vma=False,
    )
```

```python
import functools
import math

import jax
import jax.numpy as jnp
from jax import lax
from jax.experimental import pallas as pl
from jax.experimental.pallas import tpu as pltpu
from jax.sharding import PartitionSpec as P

MESH = pl.DeviceIdType.MESH
FACE = 4
SUBLANES = 16
LANES = 128
VMEM_BYTES = 60 * 1024 * 1024


def flip(index, offset):
    result, bit = index, 1
    while bit <= offset:
        if offset & bit:
            result = result + bit - 2 * bit * ((index // bit) % 2)
        bit *= 2
    return result


def silu_slope(pre_act):
    sigmoid_value = jax.nn.sigmoid(pre_act)
    return sigmoid_value * (1.0 + pre_act * (1.0 - sigmoid_value))


class Sends:
    def __init__(self):
        self.started = []

    def start(self, src, dst, send_sem, recv_sem, target):
        copy = pltpu.make_async_remote_copy(
            src_ref=src, dst_ref=dst, send_sem=send_sem, recv_sem=recv_sem,
            device_id=target, device_id_type=MESH,
        )
        copy.start()
        self.started.append(copy)

    def finish(self):
        for copy in self.started:
            copy.wait_send()


def arrived(ref, send_sem, recv_sem, target):
    pltpu.make_async_remote_copy(
        src_ref=ref, dst_ref=ref, send_sem=send_sem, recv_sem=recv_sem,
        device_id=target, device_id_type=MESH,
    ).wait_recv()


def kernel(
    n_dom, n_rep, inv_scale,
    columns_ref, features_hbm, values_hbm, weight_hbm, cotangent_hbm,
    feature_grad_ref, weight_grad_ref,
    values_ref, weight_ref, cotangent_ref, panels, grad_panels, part_out, part_in,
    weight_part, weight_in1, weight_sum1, weight_in2, weight_sum2, weight_in3, weight_out,
    local_sem, line_send, line_recv, face_send, face_recv,
    part_send, part_recv, weight_send, weight_recv,
):
    rows = cotangent_ref.shape[0]
    rounds = values_ref.shape[0]
    line = n_dom // FACE
    dom, rep = lax.axis_index("dom"), lax.axis_index("rep")
    z, face = dom // FACE, dom % FACE

    def panel_at(z_at, face_at):
        return z_at * FACE + face_at

    line_ids = [panel_at(flip(z, k), face) for k in range(line)]
    face_ids = [panel_at(z, flip(face, j)) for j in range(FACE)]
    rep_ids = [lax.rem(rep + k, n_rep) for k in range(n_rep)]
    from_rep_ids = [lax.rem(rep - k + n_rep, n_rep) for k in range(n_rep)]
    line_to = [{"dom": i} for i in line_ids]
    face_to = [{"dom": i} for i in face_ids]
    rep_to = [{"rep": i} for i in rep_ids]

    local = [
        pltpu.make_async_copy(src, dst, local_sem.at[i])
        for i, (src, dst) in enumerate((
            (features_hbm, panels.at[dom]),
            (values_hbm.at[0], values_ref),
            (weight_hbm, weight_ref),
            (cotangent_hbm, cotangent_ref),
        ))
    ]
    for copy in local:
        copy.start()

    barrier = pltpu.get_barrier_semaphore()
    partners = line_to[1:] + face_to[1:] + rep_to[1:]
    for target in partners:
        pl.semaphore_signal(barrier, inc=1, device_id=target, device_id_type=MESH)
    local[0].wait()
    pl.semaphore_wait(barrier, len(partners))

    sends = Sends()

    def gather(which, held):
        def along(k):
            own = held.at[dom]
            sends.start(own, own, line_send.at[which, k - 1], line_recv.at[which, k - 1], line_to[k])

        def over_face(k):
            piece = held.at[line_ids[k]]
            for j in (3, 1, 2):
                slot = (which, j - 1, k)
                sends.start(piece, piece, face_send.at[slot], face_recv.at[slot], face_to[j])

        def begin():
            for k in range(1, line):
                along(k)
            over_face(0)

        def middle(k):
            arrived(held.at[line_ids[k]], line_send.at[which, k - 1], line_recv.at[which, k - 1], line_to[k])
            over_face(k)

        def finish():
            for k in range(line):
                for j in range(1, FACE):
                    slot = (which, j - 1, k)
                    panel = held.at[panel_at(flip(z, k), flip(face, j))]
                    arrived(panel, face_send.at[slot], face_recv.at[slot], face_to[j])

        return [begin] + [functools.partial(middle, k) for k in range(1, line)] + [finish]

    def block_product(held, a):
        left = jnp.concatenate([values_ref[t, a] for t in range(rounds)], axis=1)
        right = jnp.concatenate([held[columns_ref[0, a, t]] for t in range(rounds)], axis=0)
        return jnp.dot(left, right, preferred_element_type=jnp.float32)

    def panel_start(which, held):
        for k in range(1, n_rep):
            part_out[which, k - 1] = block_product(held, rep_ids[k])
            sends.start(
                part_out.at[which, k - 1], part_in.at[which, k - 1],
                part_send.at[which, k - 1], part_recv.at[which, k - 1], rep_to[k],
            )
        return block_product(held, rep)

    def panel_end(which, total):
        for k in range(1, n_rep):
            arrived(
                part_in.at[which, k - 1], part_send.at[which, k - 1],
                part_recv.at[which, k - 1], rep_to[k],
            )
            total = total + part_in[which, k - 1]
        return total.astype(jnp.bfloat16)

    for step in gather(0, panels):
        step()
    for copy in local[1:]:
        copy.wait()
    hidden = panel_end(0, panel_start(0, panels))

    weight = weight_ref[...]
    pre_act = jnp.dot(hidden, weight, preferred_element_type=jnp.float32)
    grad_pre = (cotangent_ref[...].astype(jnp.float32) * silu_slope(pre_act)).astype(jnp.bfloat16)
    grad_panels[dom] = lax.dot_general(
        grad_pre, weight, (((1,), (1,)), ((), ())), preferred_element_type=jnp.float32
    ).astype(jnp.bfloat16)
    back = gather(1, grad_panels)
    back[0]()

    wide = weight.shape[0]
    rep_rows = wide // n_rep
    face_rows = rep_rows // FACE
    line_rows, line_columns = 2 * face_rows // line, wide // 2
    rep_base = rep * rep_rows
    face_base = rep_base + face * face_rows
    sem_at = [0]

    def weight_sems(count):
        base = sem_at[0]
        sem_at[0] += count - 1
        return [(weight_send.at[base + k - 1], weight_recv.at[base + k - 1]) for k in range(1, count)]

    def span(start, size):
        return (pl.ds(pl.multiple_of(start, SUBLANES), size),)

    def tile(start, z_at):
        return (
            pl.ds(pl.multiple_of(start + (z_at // 2) * line_rows, SUBLANES), line_rows),
            pl.ds(pl.multiple_of((z_at % 2) * line_columns, LANES), line_columns),
        )

    def exchange(out_ref, in_ref, targets, pieces):
        sems = weight_sems(len(targets))
        for k in range(1, len(targets)):
            sends.start(out_ref.at[pieces[k]], in_ref.at[k - 1], *sems[k - 1], targets[k])
        return sems

    def take(in_ref, sems, targets, total):
        for k in range(1, len(targets)):
            arrived(in_ref.at[k - 1], *sems[k - 1], targets[k])
            total = total + in_ref[k - 1]
        return total

    def share(piece, targets):
        sems = weight_sems(len(targets))
        for k in range(1, len(targets)):
            sends.start(weight_out.at[piece], weight_out.at[piece], *sems[k - 1], targets[k])
        return sems

    def collect(pieces, sems, targets):
        for k in range(1, len(targets)):
            arrived(weight_out.at[pieces[k]], *sems[k - 1], targets[k])

    line_z = [flip(z, k) for k in range(line)]
    face_f = [flip(face, j) for j in range(FACE)]

    weight_part[...] = lax.dot_general(
        hidden, grad_pre, (((0,), (0,)), ((), ())), preferred_element_type=jnp.float32
    )
    sems1 = exchange(weight_part, weight_in1, rep_to, [span(i * rep_rows, rep_rows) for i in rep_ids])
    weight_sum1[...] = take(weight_in1, sems1, rep_to, weight_part[span(rep_base, rep_rows)])
    sems2 = exchange(weight_sum1, weight_in2, face_to, [span(f * face_rows, face_rows) for f in face_f])
    back[1]()
    weight_sum2[...] = take(weight_in2, sems2, face_to, weight_sum1[span(face * face_rows, face_rows)])
    sems3 = exchange(weight_sum2, weight_in3, line_to, [tile(0, i) for i in line_z])
    for step in back[2:-1]:
        step()
    own_sum = take(weight_in3, sems3, line_to, weight_sum2[tile(0, z)])
    weight_out[tile(face_base, z)] = (own_sum * inv_scale).astype(jnp.bfloat16)
    sems4 = share(tile(face_base, z), line_to)
    collect([tile(face_base, i) for i in line_z], sems4, line_to)
    sems5 = share(span(face_base, face_rows), face_to)
    back[-1]()

    total = panel_start(1, grad_panels)
    collect([span(rep_base + f * face_rows, face_rows) for f in face_f], sems5, face_to)
    sems6 = share(span(rep_base, rep_rows), rep_to)
    feature_grad_ref[...] = panel_end(1, total)
    collect([span(i * rep_rows, rep_rows) for i in from_rep_ids], sems6, rep_to)
    weight_grad_ref[...] = weight_out[...].astype(jnp.float32)
    sends.finish()


def kernel_shards(features, block_values, block_columns, weight, cotangent):
    n_dom, n_rep = lax.axis_size("dom"), lax.axis_size("rep")
    rows, width = features.shape
    wide = weight.shape[0]
    line = n_dom // FACE
    rep_rows = wide // n_rep
    face_rows = rep_rows // FACE
    inv_scale = 1.0 / math.sqrt(rows * n_dom * n_rep)
    weight_copies = 2 * ((n_rep - 1) + (line - 1) + (FACE - 1))
    parts, steps = max(n_rep - 1, 1), max(line - 1, 1)
    vmem = pl.BlockSpec(memory_space=pltpu.VMEM)
    hbm = pl.BlockSpec(memory_space=pl.ANY)
    dma = pltpu.SemaphoreType.DMA
    face_slots = (2, FACE - 1, line)
    line_slots = (2, steps)
    return pl.pallas_call(
        functools.partial(kernel, n_dom, n_rep, inv_scale),
        out_shape=(
            pltpu.VMEM((rows, width), jnp.bfloat16),
            pltpu.VMEM(weight.shape, jnp.float32),
        ),
        in_specs=[pl.BlockSpec(memory_space=pltpu.SMEM)] + [hbm] * 4,
        out_specs=(vmem, vmem),
        scratch_shapes=[
            pltpu.VMEM(block_values.shape[1:], jnp.bfloat16),
            pltpu.VMEM(weight.shape, jnp.bfloat16),
            pltpu.VMEM(cotangent.shape, jnp.bfloat16),
            pltpu.VMEM((n_dom, rows, width), jnp.bfloat16),
            pltpu.VMEM((n_dom, rows, width), jnp.bfloat16),
            pltpu.VMEM((2, parts, rows, width), jnp.float32),
            pltpu.VMEM((2, parts, rows, width), jnp.float32),
            pltpu.VMEM(weight.shape, jnp.float32),
            pltpu.VMEM((parts, rep_rows, wide), jnp.float32),
            pltpu.VMEM((rep_rows, wide), jnp.float32),
            pltpu.VMEM((FACE - 1, face_rows, wide), jnp.float32),
            pltpu.VMEM((face_rows, wide), jnp.float32),
            pltpu.VMEM((steps, 2 * face_rows // line, wide // 2), jnp.float32),
            pltpu.VMEM(weight.shape, jnp.bfloat16),
            dma((4,)),
            dma(line_slots), dma(line_slots),
            dma(face_slots), dma(face_slots),
            dma((2, parts)), dma((2, parts)),
            dma((weight_copies,)), dma((weight_copies,)),
        ],
        compiler_params=pltpu.CompilerParams(
            collective_id=0, has_side_effects=True, vmem_limit_bytes=VMEM_BYTES
        ),
    )(jnp.swapaxes(block_columns, 1, 2), features, block_values, weight, cotangent)


def panel_product(values, columns, gathered, block_rows):
    panel_count = gathered.shape[0] // block_rows
    panels = gathered.reshape(panel_count, block_rows, gathered.shape[1])
    picked = panels[columns]
    summed = jnp.einsum("taij,tajf->aif", values, picked, preferred_element_type=jnp.float32)
    return summed.reshape(-1, summed.shape[-1])


def plain_shards(features, block_values, block_columns, weight, cotangent):
    block_rows = features.shape[0]
    values, columns = block_values[0], block_columns[0]
    gathered = lax.all_gather(features, "dom", axis=0, tiled=True)
    inv_scale = 1.0 / math.sqrt(gathered.shape[0] * lax.axis_size("rep"))
    partial_value = panel_product(values, columns, gathered, block_rows)
    hidden = lax.psum_scatter(partial_value, "rep", scatter_dimension=0, tiled=True).astype(jnp.bfloat16)
    pre_act = jnp.dot(hidden, weight, preferred_element_type=jnp.float32)
    grad_pre = (cotangent.astype(jnp.float32) * silu_slope(pre_act)).astype(jnp.bfloat16)
    hidden_grad = jnp.einsum(
        "rg,fg->rf", grad_pre, weight, preferred_element_type=jnp.float32
    ).astype(jnp.bfloat16)
    weight_part = jnp.einsum("rf,rg->fg", hidden, grad_pre, preferred_element_type=jnp.float32)
    weight_grad = lax.psum(weight_part, ("dom", "rep")) * inv_scale
    grad_rows = lax.all_gather(hidden_grad, "dom", axis=0, tiled=True)
    back_partial = panel_product(values, columns, grad_rows, block_rows)
    feature_grad = lax.psum_scatter(back_partial, "rep", scatter_dimension=0, tiled=True)
    return (feature_grad.astype(jnp.bfloat16), weight_grad)


def shards(features, block_values, block_columns, weight, cotangent):
    n_dom, n_rep = lax.axis_size("dom"), lax.axis_size("rep")
    line = n_dom // FACE
    splits = (
        n_dom % FACE == 0
        and line & (line - 1) == 0
        and line > 1
        and weight.shape[0] % (2 * SUBLANES * line * n_rep) == 0
        and weight.shape[0] % (2 * LANES) == 0
        and features.shape[0] % SUBLANES == 0
    )
    body = kernel_shards if splits else plain_shards
    return body(features, block_values, block_columns, weight, cotangent)


def solution(mesh):
    return jax.shard_map(
        shards,
        mesh=mesh,
        in_specs=(
            P(("dom", "rep"), None),
            P(("dom", "rep"), None, None, None, None),
            P(("dom", "rep"), None, None),
            P(),
            P(("dom", "rep"), None),
        ),
        out_specs=(P(("dom", "rep"), None), P()),
        check_vma=False,
    )
```

```python
import functools
import math

import jax
import jax.numpy as jnp
from jax import lax
from jax.experimental import pallas as pl
from jax.experimental.pallas import tpu as pltpu
from jax.sharding import PartitionSpec as P

MESH = pl.DeviceIdType.MESH
FACE = 4
SUBLANES = 16
LANES = 128
VMEM_BYTES = 60 * 1024 * 1024


def flip(index, offset):
    result, bit = index, 1
    while bit <= offset:
        if offset & bit:
            result = result + bit - 2 * bit * ((index // bit) % 2)
        bit *= 2
    return result


def silu_slope(pre_act):
    sigmoid_value = jax.nn.sigmoid(pre_act)
    return sigmoid_value * (1.0 + pre_act * (1.0 - sigmoid_value))


class Sends:
    def __init__(self):
        self.started = []

    def start(self, src, dst, send_sem, recv_sem, target):
        copy = pltpu.make_async_remote_copy(
            src_ref=src, dst_ref=dst, send_sem=send_sem, recv_sem=recv_sem,
            device_id=target, device_id_type=MESH,
        )
        copy.start()
        self.started.append(copy)

    def finish(self):
        for copy in self.started:
            copy.wait_send()


def arrived(ref, send_sem, recv_sem, target):
    pltpu.make_async_remote_copy(
        src_ref=ref, dst_ref=ref, send_sem=send_sem, recv_sem=recv_sem,
        device_id=target, device_id_type=MESH,
    ).wait_recv()


def kernel(
    n_dom, n_rep, inv_scale,
    columns_ref, features_hbm, values_hbm, weight_hbm, cotangent_hbm,
    feature_grad_ref, weight_grad_ref,
    values_ref, weight_ref, cotangent_ref, panels, grad_panels, part_out, part_in,
    weight_part, weight_in1, weight_sum1, weight_in2, weight_sum2, weight_in3, weight_out,
    local_sem, line_send, line_recv, face_send, face_recv,
    part_send, part_recv, weight_send, weight_recv,
):
    rows = cotangent_ref.shape[0]
    rounds = values_ref.shape[0]
    line = n_dom // FACE
    dom, rep = lax.axis_index("dom"), lax.axis_index("rep")
    z, face = dom // FACE, dom % FACE

    def panel_at(z_at, face_at):
        return z_at * FACE + face_at

    line_ids = [panel_at(flip(z, k), face) for k in range(line)]
    face_ids = [panel_at(z, flip(face, j)) for j in range(FACE)]
    rep_ids = [lax.rem(rep + k, n_rep) for k in range(n_rep)]
    from_rep_ids = [lax.rem(rep - k + n_rep, n_rep) for k in range(n_rep)]
    line_to = [{"dom": i} for i in line_ids]
    face_to = [{"dom": i} for i in face_ids]
    rep_to = [{"rep": i} for i in rep_ids]

    local = [
        pltpu.make_async_copy(src, dst, local_sem.at[i])
        for i, (src, dst) in enumerate((
            (features_hbm, panels.at[dom]),
            (values_hbm.at[0], values_ref),
            (weight_hbm, weight_ref),
            (cotangent_hbm, cotangent_ref),
        ))
    ]
    for copy in local:
        copy.start()

    barrier = pltpu.get_barrier_semaphore()
    partners = line_to[1:] + face_to[1:] + rep_to[1:]
    for target in partners:
        pl.semaphore_signal(barrier, inc=1, device_id=target, device_id_type=MESH)
    local[0].wait()
    pl.semaphore_wait(barrier, len(partners))

    sends = Sends()

    def gather(which, held):
        def along(k):
            own = held.at[dom]
            sends.start(own, own, line_send.at[which, k - 1], line_recv.at[which, k - 1], line_to[k])

        def over_face(k):
            piece = held.at[line_ids[k]]
            for j in (3, 1, 2):
                slot = (which, j - 1, k)
                sends.start(piece, piece, face_send.at[slot], face_recv.at[slot], face_to[j])

        def begin():
            for k in range(line - 1, 0, -1):
                along(k)
            over_face(0)

        def middle(k):
            arrived(held.at[line_ids[k]], line_send.at[which, k - 1], line_recv.at[which, k - 1], line_to[k])
            over_face(k)

        def finish():
            for k in range(line):
                for j in range(1, FACE):
                    slot = (which, j - 1, k)
                    panel = held.at[panel_at(flip(z, k), flip(face, j))]
                    arrived(panel, face_send.at[slot], face_recv.at[slot], face_to[j])

        return [begin] + [functools.partial(middle, k) for k in range(1, line)] + [finish]

    def block_product(held, a):
        left = jnp.concatenate([values_ref[t, a] for t in range(rounds)], axis=1)
        right = jnp.concatenate([held[columns_ref[0, a, t]] for t in range(rounds)], axis=0)
        return jnp.dot(left, right, preferred_element_type=jnp.float32)

    def panel_start(which, held):
        for k in range(1, n_rep):
            part_out[which, k - 1] = block_product(held, rep_ids[k])
            sends.start(
                part_out.at[which, k - 1], part_in.at[which, k - 1],
                part_send.at[which, k - 1], part_recv.at[which, k - 1], rep_to[k],
            )
        return block_product(held, rep)

    def panel_end(which, total):
        for k in range(1, n_rep):
            arrived(
                part_in.at[which, k - 1], part_send.at[which, k - 1],
                part_recv.at[which, k - 1], rep_to[k],
            )
            total = total + part_in[which, k - 1]
        return total.astype(jnp.bfloat16)

    for step in gather(0, panels):
        step()
    for copy in local[1:]:
        copy.wait()
    hidden = panel_end(0, panel_start(0, panels))

    weight = weight_ref[...]
    pre_act = jnp.dot(hidden, weight, preferred_element_type=jnp.float32)
    grad_pre = (cotangent_ref[...].astype(jnp.float32) * silu_slope(pre_act)).astype(jnp.bfloat16)
    grad_panels[dom] = lax.dot_general(
        grad_pre, weight, (((1,), (1,)), ((), ())), preferred_element_type=jnp.float32
    ).astype(jnp.bfloat16)
    back = gather(1, grad_panels)
    back[0]()

    wide = weight.shape[0]
    rep_rows = wide // n_rep
    face_rows = rep_rows // FACE
    line_rows, line_columns = 2 * face_rows // line, wide // 2
    rep_base = rep * rep_rows
    face_base = rep_base + face * face_rows
    sem_at = [0]

    def weight_sems(count):
        base = sem_at[0]
        sem_at[0] += count - 1
        return [(weight_send.at[base + k - 1], weight_recv.at[base + k - 1]) for k in range(1, count)]

    def span(start, size):
        return (pl.ds(pl.multiple_of(start, SUBLANES), size),)

    def tile(start, z_at):
        return (
            pl.ds(pl.multiple_of(start + (z_at // 2) * line_rows, SUBLANES), line_rows),
            pl.ds(pl.multiple_of((z_at % 2) * line_columns, LANES), line_columns),
        )

    def exchange(out_ref, in_ref, targets, pieces):
        sems = weight_sems(len(targets))
        for k in range(1, len(targets)):
            sends.start(out_ref.at[pieces[k]], in_ref.at[k - 1], *sems[k - 1], targets[k])
        return sems

    def take(in_ref, sems, targets, total):
        for k in range(1, len(targets)):
            arrived(in_ref.at[k - 1], *sems[k - 1], targets[k])
            total = total + in_ref[k - 1]
        return total

    def share(piece, targets):
        sems = weight_sems(len(targets))
        for k in range(1, len(targets)):
            sends.start(weight_out.at[piece], weight_out.at[piece], *sems[k - 1], targets[k])
        return sems

    def collect(pieces, sems, targets):
        for k in range(1, len(targets)):
            arrived(weight_out.at[pieces[k]], *sems[k - 1], targets[k])

    line_z = [flip(z, k) for k in range(line)]
    face_f = [flip(face, j) for j in range(FACE)]

    weight_part[...] = lax.dot_general(
        hidden, grad_pre, (((0,), (0,)), ((), ())), preferred_element_type=jnp.float32
    )
    sems1 = exchange(weight_part, weight_in1, rep_to, [span(i * rep_rows, rep_rows) for i in rep_ids])
    weight_sum1[...] = take(weight_in1, sems1, rep_to, weight_part[span(rep_base, rep_rows)])
    sems2 = exchange(weight_sum1, weight_in2, face_to, [span(f * face_rows, face_rows) for f in face_f])
    back[1]()
    weight_sum2[...] = take(weight_in2, sems2, face_to, weight_sum1[span(face * face_rows, face_rows)])
    sems3 = exchange(weight_sum2, weight_in3, line_to, [tile(0, i) for i in line_z])
    for step in back[2:-1]:
        step()
    own_sum = take(weight_in3, sems3, line_to, weight_sum2[tile(0, z)])
    weight_out[tile(face_base, z)] = (own_sum * inv_scale).astype(jnp.bfloat16)
    sems4 = share(tile(face_base, z), line_to)
    collect([tile(face_base, i) for i in line_z], sems4, line_to)
    sems5 = share(span(face_base, face_rows), face_to)
    back[-1]()

    total = panel_start(1, grad_panels)
    collect([span(rep_base + f * face_rows, face_rows) for f in face_f], sems5, face_to)
    sems6 = share(span(rep_base, rep_rows), rep_to)
    feature_grad_ref[...] = panel_end(1, total)
    collect([span(i * rep_rows, rep_rows) for i in from_rep_ids], sems6, rep_to)
    weight_grad_ref[...] = weight_out[...].astype(jnp.float32)
    sends.finish()


def kernel_shards(features, block_values, block_columns, weight, cotangent):
    n_dom, n_rep = lax.axis_size("dom"), lax.axis_size("rep")
    rows, width = features.shape
    wide = weight.shape[0]
    line = n_dom // FACE
    rep_rows = wide // n_rep
    face_rows = rep_rows // FACE
    inv_scale = 1.0 / math.sqrt(rows * n_dom * n_rep)
    weight_copies = 2 * ((n_rep - 1) + (line - 1) + (FACE - 1))
    parts, steps = max(n_rep - 1, 1), max(line - 1, 1)
    vmem = pl.BlockSpec(memory_space=pltpu.VMEM)
    hbm = pl.BlockSpec(memory_space=pl.ANY)
    dma = pltpu.SemaphoreType.DMA
    face_slots = (2, FACE - 1, line)
    line_slots = (2, steps)
    return pl.pallas_call(
        functools.partial(kernel, n_dom, n_rep, inv_scale),
        out_shape=(
            pltpu.VMEM((rows, width), jnp.bfloat16),
            pltpu.VMEM(weight.shape, jnp.float32),
        ),
        in_specs=[pl.BlockSpec(memory_space=pltpu.SMEM)] + [hbm] * 4,
        out_specs=(vmem, vmem),
        scratch_shapes=[
            pltpu.VMEM(block_values.shape[1:], jnp.bfloat16),
            pltpu.VMEM(weight.shape, jnp.bfloat16),
            pltpu.VMEM(cotangent.shape, jnp.bfloat16),
            pltpu.VMEM((n_dom, rows, width), jnp.bfloat16),
            pltpu.VMEM((n_dom, rows, width), jnp.bfloat16),
            pltpu.VMEM((2, parts, rows, width), jnp.float32),
            pltpu.VMEM((2, parts, rows, width), jnp.float32),
            pltpu.VMEM(weight.shape, jnp.float32),
            pltpu.VMEM((parts, rep_rows, wide), jnp.float32),
            pltpu.VMEM((rep_rows, wide), jnp.float32),
            pltpu.VMEM((FACE - 1, face_rows, wide), jnp.float32),
            pltpu.VMEM((face_rows, wide), jnp.float32),
            pltpu.VMEM((steps, 2 * face_rows // line, wide // 2), jnp.float32),
            pltpu.VMEM(weight.shape, jnp.bfloat16),
            dma((4,)),
            dma(line_slots), dma(line_slots),
            dma(face_slots), dma(face_slots),
            dma((2, parts)), dma((2, parts)),
            dma((weight_copies,)), dma((weight_copies,)),
        ],
        compiler_params=pltpu.CompilerParams(
            collective_id=0, has_side_effects=True, vmem_limit_bytes=VMEM_BYTES
        ),
    )(jnp.swapaxes(block_columns, 1, 2), features, block_values, weight, cotangent)


def panel_product(values, columns, gathered, block_rows):
    panel_count = gathered.shape[0] // block_rows
    panels = gathered.reshape(panel_count, block_rows, gathered.shape[1])
    picked = panels[columns]
    summed = jnp.einsum("taij,tajf->aif", values, picked, preferred_element_type=jnp.float32)
    return summed.reshape(-1, summed.shape[-1])


def plain_shards(features, block_values, block_columns, weight, cotangent):
    block_rows = features.shape[0]
    values, columns = block_values[0], block_columns[0]
    gathered = lax.all_gather(features, "dom", axis=0, tiled=True)
    inv_scale = 1.0 / math.sqrt(gathered.shape[0] * lax.axis_size("rep"))
    partial_value = panel_product(values, columns, gathered, block_rows)
    hidden = lax.psum_scatter(partial_value, "rep", scatter_dimension=0, tiled=True).astype(jnp.bfloat16)
    pre_act = jnp.dot(hidden, weight, preferred_element_type=jnp.float32)
    grad_pre = (cotangent.astype(jnp.float32) * silu_slope(pre_act)).astype(jnp.bfloat16)
    hidden_grad = jnp.einsum(
        "rg,fg->rf", grad_pre, weight, preferred_element_type=jnp.float32
    ).astype(jnp.bfloat16)
    weight_part = jnp.einsum("rf,rg->fg", hidden, grad_pre, preferred_element_type=jnp.float32)
    weight_grad = lax.psum(weight_part, ("dom", "rep")) * inv_scale
    grad_rows = lax.all_gather(hidden_grad, "dom", axis=0, tiled=True)
    back_partial = panel_product(values, columns, grad_rows, block_rows)
    feature_grad = lax.psum_scatter(back_partial, "rep", scatter_dimension=0, tiled=True)
    return (feature_grad.astype(jnp.bfloat16), weight_grad)


def shards(features, block_values, block_columns, weight, cotangent):
    n_dom, n_rep = lax.axis_size("dom"), lax.axis_size("rep")
    line = n_dom // FACE
    splits = (
        n_dom % FACE == 0
        and line & (line - 1) == 0
        and line > 1
        and weight.shape[0] % (2 * SUBLANES * line * n_rep) == 0
        and weight.shape[0] % (2 * LANES) == 0
        and features.shape[0] % SUBLANES == 0
    )
    body = kernel_shards if splits else plain_shards
    return body(features, block_values, block_columns, weight, cotangent)


def solution(mesh):
    return jax.shard_map(
        shards,
        mesh=mesh,
        in_specs=(
            P(("dom", "rep"), None),
            P(("dom", "rep"), None, None, None, None),
            P(("dom", "rep"), None, None),
            P(),
            P(("dom", "rep"), None),
        ),
        out_specs=(P(("dom", "rep"), None), P()),
        check_vma=False,
    )
```

```python
import functools
import math

import jax
import jax.numpy as jnp
from jax import lax
from jax.experimental import pallas as pl
from jax.experimental.pallas import tpu as pltpu
from jax.sharding import PartitionSpec as P

MESH = pl.DeviceIdType.MESH
FACE = 4
SUBLANES = 16
LANES = 128
VMEM_BYTES = 60 * 1024 * 1024


def flip(index, offset):
    result, bit = index, 1
    while bit <= offset:
        if offset & bit:
            result = result + bit - 2 * bit * ((index // bit) % 2)
        bit *= 2
    return result


def silu_slope(pre_act):
    sigmoid_value = jax.nn.sigmoid(pre_act)
    return sigmoid_value * (1.0 + pre_act * (1.0 - sigmoid_value))


class Sends:
    def __init__(self):
        self.started = []

    def start(self, src, dst, send_sem, recv_sem, target):
        copy = pltpu.make_async_remote_copy(
            src_ref=src, dst_ref=dst, send_sem=send_sem, recv_sem=recv_sem,
            device_id=target, device_id_type=MESH,
        )
        copy.start()
        self.started.append(copy)

    def finish(self):
        for copy in self.started:
            copy.wait_send()


def arrived(ref, send_sem, recv_sem, target):
    pltpu.make_async_remote_copy(
        src_ref=ref, dst_ref=ref, send_sem=send_sem, recv_sem=recv_sem,
        device_id=target, device_id_type=MESH,
    ).wait_recv()


def kernel(
    n_dom, n_rep, inv_scale,
    columns_ref, features_hbm, values_hbm, weight_hbm, cotangent_hbm,
    feature_grad_ref, weight_grad_ref,
    values_ref, weight_ref, cotangent_ref, panels, grad_panels, part_out, part_in,
    weight_part, weight_in1, weight_sum1, weight_in2, weight_sum2, weight_in3, weight_out,
    local_sem, line_send, line_recv, face_send, face_recv,
    part_send, part_recv, weight_send, weight_recv,
):
    rows = cotangent_ref.shape[0]
    rounds = values_ref.shape[0]
    line = n_dom // FACE
    dom, rep = lax.axis_index("dom"), lax.axis_index("rep")
    z, face = dom // FACE, dom % FACE

    def panel_at(z_at, face_at):
        return z_at * FACE + face_at

    line_ids = [panel_at(flip(z, k), face) for k in range(line)]
    face_ids = [panel_at(z, flip(face, j)) for j in range(FACE)]
    rep_ids = [lax.rem(rep + k, n_rep) for k in range(n_rep)]
    from_rep_ids = [lax.rem(rep - k + n_rep, n_rep) for k in range(n_rep)]
    line_to = [{"dom": i} for i in line_ids]
    face_to = [{"dom": i} for i in face_ids]
    rep_to = [{"rep": i} for i in rep_ids]

    local = [
        pltpu.make_async_copy(src, dst, local_sem.at[i])
        for i, (src, dst) in enumerate((
            (features_hbm, panels.at[dom]),
            (values_hbm.at[0], values_ref),
            (weight_hbm, weight_ref),
            (cotangent_hbm, cotangent_ref),
        ))
    ]
    for copy in local:
        copy.start()

    barrier = pltpu.get_barrier_semaphore()
    partners = line_to[1:] + face_to[1:] + rep_to[1:]
    for target in partners:
        pl.semaphore_signal(barrier, inc=1, device_id=target, device_id_type=MESH)
    local[0].wait()
    pl.semaphore_wait(barrier, len(partners))

    sends = Sends()

    def gather(which, held):
        def along(k):
            own = held.at[dom]
            sends.start(own, own, line_send.at[which, k - 1], line_recv.at[which, k - 1], line_to[k])

        def over_face(k):
            piece = held.at[line_ids[k]]
            for j in (1, 2, 3):
                slot = (which, j - 1, k)
                sends.start(piece, piece, face_send.at[slot], face_recv.at[slot], face_to[j])

        def begin():
            for k in range(1, line):
                along(k)
            over_face(0)

        def middle(k):
            arrived(held.at[line_ids[k]], line_send.at[which, k - 1], line_recv.at[which, k - 1], line_to[k])
            over_face(k)

        def finish():
            for k in range(line):
                for j in range(1, FACE):
                    slot = (which, j - 1, k)
                    panel = held.at[panel_at(flip(z, k), flip(face, j))]
                    arrived(panel, face_send.at[slot], face_recv.at[slot], face_to[j])

        return [begin] + [functools.partial(middle, k) for k in range(1, line)] + [finish]

    def block_product(held, a):
        left = jnp.concatenate([values_ref[t, a] for t in range(rounds)], axis=1)
        right = jnp.concatenate([held[columns_ref[0, a, t]] for t in range(rounds)], axis=0)
        return jnp.dot(left, right, preferred_element_type=jnp.float32)

    def panel_start(which, held):
        for k in range(1, n_rep):
            part_out[which, k - 1] = block_product(held, rep_ids[k])
            sends.start(
                part_out.at[which, k - 1], part_in.at[which, k - 1],
                part_send.at[which, k - 1], part_recv.at[which, k - 1], rep_to[k],
            )
        return block_product(held, rep)

    def panel_end(which, total):
        for k in range(1, n_rep):
            arrived(
                part_in.at[which, k - 1], part_send.at[which, k - 1],
                part_recv.at[which, k - 1], rep_to[k],
            )
            total = total + part_in[which, k - 1]
        return total.astype(jnp.bfloat16)

    for step in gather(0, panels):
        step()
    for copy in local[1:]:
        copy.wait()
    hidden = panel_end(0, panel_start(0, panels))

    weight = weight_ref[...]
    pre_act = jnp.dot(hidden, weight, preferred_element_type=jnp.float32)
    grad_pre = (cotangent_ref[...].astype(jnp.float32) * silu_slope(pre_act)).astype(jnp.bfloat16)
    grad_panels[dom] = lax.dot_general(
        grad_pre, weight, (((1,), (1,)), ((), ())), preferred_element_type=jnp.float32
    ).astype(jnp.bfloat16)
    back = gather(1, grad_panels)
    back[0]()

    wide = weight.shape[0]
    rep_rows = wide // n_rep
    face_rows = rep_rows // FACE
    line_rows, line_columns = 2 * face_rows // line, wide // 2
    rep_base = rep * rep_rows
    face_base = rep_base + face * face_rows
    sem_at = [0]

    def weight_sems(count):
        base = sem_at[0]
        sem_at[0] += count - 1
        return [(weight_send.at[base + k - 1], weight_recv.at[base + k - 1]) for k in range(1, count)]

    def span(start, size):
        return (pl.ds(pl.multiple_of(start, SUBLANES), size),)

    def tile(start, z_at):
        return (
            pl.ds(pl.multiple_of(start + (z_at // 2) * line_rows, SUBLANES), line_rows),
            pl.ds(pl.multiple_of((z_at % 2) * line_columns, LANES), line_columns),
        )

    def exchange(out_ref, in_ref, targets, pieces):
        sems = weight_sems(len(targets))
        for k in range(1, len(targets)):
            sends.start(out_ref.at[pieces[k]], in_ref.at[k - 1], *sems[k - 1], targets[k])
        return sems

    def take(in_ref, sems, targets, total):
        for k in range(1, len(targets)):
            arrived(in_ref.at[k - 1], *sems[k - 1], targets[k])
            total = total + in_ref[k - 1]
        return total

    def share(piece, targets):
        sems = weight_sems(len(targets))
        for k in range(1, len(targets)):
            sends.start(weight_out.at[piece], weight_out.at[piece], *sems[k - 1], targets[k])
        return sems

    def collect(pieces, sems, targets):
        for k in range(1, len(targets)):
            arrived(weight_out.at[pieces[k]], *sems[k - 1], targets[k])

    line_z = [flip(z, k) for k in range(line)]
    face_f = [flip(face, j) for j in range(FACE)]

    weight_part[...] = lax.dot_general(
        hidden, grad_pre, (((0,), (0,)), ((), ())), preferred_element_type=jnp.float32
    )
    sems1 = exchange(weight_part, weight_in1, rep_to, [span(i * rep_rows, rep_rows) for i in rep_ids])
    weight_sum1[...] = take(weight_in1, sems1, rep_to, weight_part[span(rep_base, rep_rows)])
    sems2 = exchange(weight_sum1, weight_in2, face_to, [span(f * face_rows, face_rows) for f in face_f])
    back[1]()
    weight_sum2[...] = take(weight_in2, sems2, face_to, weight_sum1[span(face * face_rows, face_rows)])
    sems3 = exchange(weight_sum2, weight_in3, line_to, [tile(0, i) for i in line_z])
    for step in back[2:-1]:
        step()
    own_sum = take(weight_in3, sems3, line_to, weight_sum2[tile(0, z)])
    weight_out[tile(face_base, z)] = (own_sum * inv_scale).astype(jnp.bfloat16)
    sems4 = share(tile(face_base, z), line_to)
    collect([tile(face_base, i) for i in line_z], sems4, line_to)
    sems5 = share(span(face_base, face_rows), face_to)
    back[-1]()

    total = panel_start(1, grad_panels)
    collect([span(rep_base + f * face_rows, face_rows) for f in face_f], sems5, face_to)
    sems6 = share(span(rep_base, rep_rows), rep_to)
    feature_grad_ref[...] = panel_end(1, total)
    collect([span(i * rep_rows, rep_rows) for i in from_rep_ids], sems6, rep_to)
    weight_grad_ref[...] = weight_out[...].astype(jnp.float32)
    sends.finish()


def kernel_shards(features, block_values, block_columns, weight, cotangent):
    n_dom, n_rep = lax.axis_size("dom"), lax.axis_size("rep")
    rows, width = features.shape
    wide = weight.shape[0]
    line = n_dom // FACE
    rep_rows = wide // n_rep
    face_rows = rep_rows // FACE
    inv_scale = 1.0 / math.sqrt(rows * n_dom * n_rep)
    weight_copies = 2 * ((n_rep - 1) + (line - 1) + (FACE - 1))
    parts, steps = max(n_rep - 1, 1), max(line - 1, 1)
    vmem = pl.BlockSpec(memory_space=pltpu.VMEM)
    hbm = pl.BlockSpec(memory_space=pl.ANY)
    dma = pltpu.SemaphoreType.DMA
    face_slots = (2, FACE - 1, line)
    line_slots = (2, steps)
    return pl.pallas_call(
        functools.partial(kernel, n_dom, n_rep, inv_scale),
        out_shape=(
            pltpu.VMEM((rows, width), jnp.bfloat16),
            pltpu.VMEM(weight.shape, jnp.float32),
        ),
        in_specs=[pl.BlockSpec(memory_space=pltpu.SMEM)] + [hbm] * 4,
        out_specs=(vmem, vmem),
        scratch_shapes=[
            pltpu.VMEM(block_values.shape[1:], jnp.bfloat16),
            pltpu.VMEM(weight.shape, jnp.bfloat16),
            pltpu.VMEM(cotangent.shape, jnp.bfloat16),
            pltpu.VMEM((n_dom, rows, width), jnp.bfloat16),
            pltpu.VMEM((n_dom, rows, width), jnp.bfloat16),
            pltpu.VMEM((2, parts, rows, width), jnp.float32),
            pltpu.VMEM((2, parts, rows, width), jnp.float32),
            pltpu.VMEM(weight.shape, jnp.float32),
            pltpu.VMEM((parts, rep_rows, wide), jnp.float32),
            pltpu.VMEM((rep_rows, wide), jnp.float32),
            pltpu.VMEM((FACE - 1, face_rows, wide), jnp.float32),
            pltpu.VMEM((face_rows, wide), jnp.float32),
            pltpu.VMEM((steps, 2 * face_rows // line, wide // 2), jnp.float32),
            pltpu.VMEM(weight.shape, jnp.bfloat16),
            dma((4,)),
            dma(line_slots), dma(line_slots),
            dma(face_slots), dma(face_slots),
            dma((2, parts)), dma((2, parts)),
            dma((weight_copies,)), dma((weight_copies,)),
        ],
        compiler_params=pltpu.CompilerParams(
            collective_id=0, has_side_effects=True, vmem_limit_bytes=VMEM_BYTES
        ),
    )(jnp.swapaxes(block_columns, 1, 2), features, block_values, weight, cotangent)


def panel_product(values, columns, gathered, block_rows):
    panel_count = gathered.shape[0] // block_rows
    panels = gathered.reshape(panel_count, block_rows, gathered.shape[1])
    picked = panels[columns]
    summed = jnp.einsum("taij,tajf->aif", values, picked, preferred_element_type=jnp.float32)
    return summed.reshape(-1, summed.shape[-1])


def plain_shards(features, block_values, block_columns, weight, cotangent):
    block_rows = features.shape[0]
    values, columns = block_values[0], block_columns[0]
    gathered = lax.all_gather(features, "dom", axis=0, tiled=True)
    inv_scale = 1.0 / math.sqrt(gathered.shape[0] * lax.axis_size("rep"))
    partial_value = panel_product(values, columns, gathered, block_rows)
    hidden = lax.psum_scatter(partial_value, "rep", scatter_dimension=0, tiled=True).astype(jnp.bfloat16)
    pre_act = jnp.dot(hidden, weight, preferred_element_type=jnp.float32)
    grad_pre = (cotangent.astype(jnp.float32) * silu_slope(pre_act)).astype(jnp.bfloat16)
    hidden_grad = jnp.einsum(
        "rg,fg->rf", grad_pre, weight, preferred_element_type=jnp.float32
    ).astype(jnp.bfloat16)
    weight_part = jnp.einsum("rf,rg->fg", hidden, grad_pre, preferred_element_type=jnp.float32)
    weight_grad = lax.psum(weight_part, ("dom", "rep")) * inv_scale
    grad_rows = lax.all_gather(hidden_grad, "dom", axis=0, tiled=True)
    back_partial = panel_product(values, columns, grad_rows, block_rows)
    feature_grad = lax.psum_scatter(back_partial, "rep", scatter_dimension=0, tiled=True)
    return (feature_grad.astype(jnp.bfloat16), weight_grad)


def shards(features, block_values, block_columns, weight, cotangent):
    n_dom, n_rep = lax.axis_size("dom"), lax.axis_size("rep")
    line = n_dom // FACE
    splits = (
        n_dom % FACE == 0
        and line & (line - 1) == 0
        and line > 1
        and weight.shape[0] % (2 * SUBLANES * line * n_rep) == 0
        and weight.shape[0] % (2 * LANES) == 0
        and features.shape[0] % SUBLANES == 0
    )
    body = kernel_shards if splits else plain_shards
    return body(features, block_values, block_columns, weight, cotangent)


def solution(mesh):
    return jax.shard_map(
        shards,
        mesh=mesh,
        in_specs=(
            P(("dom", "rep"), None),
            P(("dom", "rep"), None, None, None, None),
            P(("dom", "rep"), None, None),
            P(),
            P(("dom", "rep"), None),
        ),
        out_specs=(P(("dom", "rep"), None), P()),
        check_vma=False,
    )
```
